256 devices in a mesh: seq: 64 (over z, x, core), section: 4 (over y).
Axes of the slice: x: 4, y: 4, z: 8, core: 2. Of those that a mesh axis runs over, the one named last changes fastest.
Arguments:
- enc_out: bfloat16 [32768, 4096], P('seq'), may hold values from -6 to 6
- span_len: int32 [64, 192], P('seq'), may hold values from 0 to 497, as said below
- skip_rows: bfloat16 [32768, 1024], P('seq', 'section'), may hold values from -6 to 6
- norm_gain: float32 [4096], replicated, may hold values from 0.1 to 1.9
- w_query: bfloat16 [4096, 2048], P(None, 'section'), may hold values from -3 to 3
- w_key: bfloat16 [4096, 512], P(None, 'section'), may hold values from -3 to 3
- w_value: bfloat16 [4096, 512], P(None, 'section'), may hold values from -0.09375 to 0.09375
- w_out: bfloat16 [2048, 1024], P('section'), may hold values from -0.125 to 0.125
- conv_kernel: float32 [31, 1024], P(None, 'section'), may hold values from -1 to 1
Outputs:
- decoded: bfloat16 [32768, 1024], P('seq', 'section')
The draws below stay inside these ranges and needn't reach their ends.
Inputs may be any that keep to these rules, and one draw needn't show every extreme that they name: `span_len`: row d lists the lengths of the spans that start in the bytes of index d of seq: its first entries are positive and sum to 512, the rest are 0. Rows hold between 16 and 192 spans and some row holds exactly 192; all rows together hold 4096 spans. Some row holds exactly 16 spans, the first of them as long as the maximum.
All inputs are finite; a program needn't handle non-finite values.
Results may differ from the reference program's by a relative error of at most 0.015.
Values may be sent and summed in bfloat16 or wider, within the bound.
No kernel may reach another device: no remote copies, remote signals or barrier semaphores. Data moves between devices by JAX's collectives and lax.ppermute only.
A program may use at most 64 MiB of HBM per device.

```python
import math
import jax
import jax.numpy as jnp
from jax import lax

DIN = 4096
DB = 1024
HEADS = 16
KVH = 4
HD = 128
KW = 31
BYTES_DEV = 512
SPANS_DEV = 64
CAP = 192
BYTES = 32768
SPANS = 4096
N_SEQ = 64


def draw_enc_out(key, part):
    key = jax.random.fold_in(key, 29)
    noise_key = jax.random.fold_in(key, 0)
    values = jnp.clip(jax.random.normal(noise_key, (BYTES, DIN), jnp.float32), -6.0, 6.0)
    return jnp.clip(values, -6.0, 6.0).astype(jnp.bfloat16)


def draw_w_query(key, part):
    key = jax.random.fold_in(key, 23)
    values = jnp.clip(jax.random.normal(key, (DIN, HEADS * HD), jnp.float32), -6.0, 6.0) * (DIN // 9) ** (-0.5)
    return jnp.clip(values, -3.0, 3.0).astype(jnp.bfloat16)


def draw_w_key(key, part):
    key = jax.random.fold_in(key, 31)
    values = jnp.clip(jax.random.normal(key, (DIN, KVH * HD), jnp.float32), -6.0, 6.0) * DIN ** (-0.5)
    return jnp.clip(values, -3.0, 3.0).astype(jnp.bfloat16)


def draw_span_len(key, part):
    key = jax.random.fold_in(key, 17)
    keys_list = jax.random.split(key, 4)
    low_count = SPANS_DEV // 4
    others = N_SEQ - 2
    spare = SPANS - CAP - low_count - others * low_count
    weights = jax.random.randint(keys_list[0], (others,), 4, 8).astype(jnp.int32)
    extra = spare * weights // jnp.sum(weights)
    leftover = spare - jnp.sum(extra)
    ranks = jax.random.permutation(keys_list[1], others)
    extra = extra + (ranks < leftover).astype(jnp.int32)
    values = jnp.concatenate([jnp.array([CAP, low_count], jnp.int32), (low_count + extra).astype(jnp.int32)])
    order = jax.random.permutation(keys_list[2], N_SEQ)
    counts = jnp.zeros((N_SEQ,), jnp.int32).at[order].set(values)
    long_flags = jnp.arange(N_SEQ) == order[1]

    def one_device(device_key, count_here, long_flag):
        spread_ranks = jax.random.permutation(device_key, BYTES_DEV - 1)
        spread_marks = spread_ranks < count_here - 1
        tail_marks = jnp.arange(BYTES_DEV - 1) >= BYTES_DEV - count_here
        marks = jnp.where(long_flag, tail_marks, spread_marks)
        is_start = jnp.concatenate([jnp.ones((1,), jnp.int32), marks.astype(jnp.int32)])
        span_of = jnp.cumsum(is_start) - 1
        slot_ids = jnp.arange(CAP, dtype=jnp.int32)
        return jnp.sum((span_of[None, :] == slot_ids[:, None]).astype(jnp.int32), axis=1)
    device_keys = jax.random.split(keys_list[3], N_SEQ)
    return jax.vmap(one_device)(device_keys, counts, long_flags).astype(jnp.int32)


def block_scale(rng, shape, pieces, smallest, largest):
    gain = 1.0
    for position, parts in pieces:
        draws = jax.random.uniform(jax.random.fold_in(jax.random.fold_in(rng, 6), position), (parts,), jnp.float32, smallest / len(pieces), largest / len(pieces))
        gain = gain * jnp.repeat(jnp.exp(draws), shape[position] // parts).reshape((-1,) + (1,) * (len(shape) - 1 - position))
    return gain


def gaussian(key, dims, spread, most, cuts=(), kind=jnp.bfloat16):
    loudness = block_scale(key, dims, cuts, -0.22, 0.18) if cuts else 1.0
    values = jax.random.normal(key, dims, jnp.float32) * spread * loudness
    return jnp.minimum(jnp.maximum(values, -most), most).astype(kind)


def setup_inputs(seed: int = 0) -> dict:
    keys = jax.random.split(jax.random.key(seed), 10)
    enc_out = draw_enc_out(jax.random.fold_in(keys[9], 71), 0)
    span_len = draw_span_len(jax.random.fold_in(keys[9], 71), 0)
    skip_rows = gaussian(keys[2], (BYTES, DB), 1.0, 6.0, ((0, 64), (1, 4)))
    norm_gain = jnp.clip(1.0 + 0.18 * jax.random.normal(keys[3], (DIN,), jnp.float32), 0.1, 1.9)
    w_query = draw_w_query(jax.random.fold_in(keys[9], 71), 0)
    w_key = draw_w_key(jax.random.fold_in(keys[9], 71), 0)
    w_value = gaussian(keys[6], (DIN, KVH * HD), DIN ** -0.5, 0.09375, ((1, 4),))
    w_out = gaussian(keys[7], (HEADS * HD, DB), (HEADS * HD) ** -0.5, 0.125, ((0, 4),))
    conv_kernel = gaussian(keys[8], (KW, DB), KW ** -0.5, 1.0, ((1, 4),), jnp.float32)
    return {"enc_out": enc_out, "span_len": span_len, "skip_rows": skip_rows, "norm_gain": norm_gain, "w_query": w_query, "w_key": w_key, "w_value": w_value, "w_out": w_out, "conv_kernel": conv_kernel}


def reference(enc_out, span_len, skip_rows, norm_gain, w_query, w_key, w_value, w_out, conv_kernel):
    is_live = span_len > 0
    counts = lax.optimization_barrier(jnp.sum(is_live.astype(jnp.int32), axis=1))
    offsets = jnp.cumsum(counts) - counts
    local_start = jnp.cumsum(span_len, axis=1) - span_len
    slot_ids = jnp.arange(CAP, dtype=jnp.int32)[None, :]
    global_ids = jnp.where(is_live, offsets[:, None] + slot_ids, SPANS).astype(jnp.int32)
    byte_start = local_start + (jnp.arange(N_SEQ, dtype=jnp.int32) * BYTES_DEV)[:, None]
    span_start = jnp.zeros((SPANS,), jnp.int32).at[global_ids.reshape(-1)].set(byte_start.reshape(-1).astype(jnp.int32), mode='drop')
    pooled = jnp.take(enc_out, span_start, axis=0).astype(jnp.float32)
    scale_rows = lax.rsqrt(lax.optimization_barrier(jnp.mean(pooled * pooled, axis=1, keepdims=True)) + 1e-05)
    normed = (pooled * scale_rows * norm_gain).astype(jnp.bfloat16)
    query_rows = jnp.dot(normed, w_query, preferred_element_type=jnp.float32).astype(jnp.bfloat16)
    key_rows = jnp.dot(normed, w_key, preferred_element_type=jnp.float32).astype(jnp.bfloat16)
    value_rows = jnp.dot(normed, w_value, preferred_element_type=jnp.float32).astype(jnp.bfloat16)
    groups = HEADS // KVH
    query_heads = query_rows.reshape(SPANS, KVH, groups, HD)
    key_heads = key_rows.reshape(SPANS, KVH, HD).astype(jnp.float32)
    value_heads = value_rows.reshape(SPANS, KVH, HD).astype(jnp.float32)
    block_rows = math.gcd(SPANS, 512)
    key_ids = jnp.arange(SPANS, dtype=jnp.int32)

    def one_block(block_index):
        first_row = (block_index * block_rows).astype(jnp.int32)
        queries = lax.dynamic_slice_in_dim(query_heads, first_row, block_rows, 0).astype(jnp.float32)
        scores = jnp.einsum('wkgd,rkd->wkgr', queries, key_heads) * HD ** (-0.5)
        query_ids = first_row + jnp.arange(block_rows, dtype=jnp.int32)
        allowed = (key_ids[None, :] <= query_ids[:, None])[:, None, None, :]
        scores = jnp.where(allowed, scores, -1e+30)
        row_max = lax.optimization_barrier(jnp.max(scores, axis=3, keepdims=True))
        weights = jnp.where(allowed, jnp.exp(scores - row_max), 0.0)
        weight_sum = lax.optimization_barrier(jnp.sum(weights, axis=3))
        rounded = weights.astype(jnp.bfloat16).astype(jnp.float32)
        summed = jnp.einsum('wkgr,rkd->wkgd', rounded, value_heads)
        return (summed / weight_sum[..., None]).reshape(block_rows, HEADS * HD).astype(jnp.bfloat16)
    attended = lax.map(one_block, jnp.arange(SPANS // block_rows, dtype=jnp.int32)).reshape(SPANS, HEADS * HD)
    inner_rows = jnp.dot(attended, w_out, preferred_element_type=jnp.float32).astype(jnp.bfloat16)
    byte_ids = jnp.arange(BYTES_DEV, dtype=jnp.int32)[None, :, None]
    covers = (byte_ids >= local_start[:, None, :]) & is_live[:, None, :]
    slot_of = lax.optimization_barrier(jnp.sum(covers.astype(jnp.int32), axis=2)) - 1
    span_of = (offsets[:, None] + slot_of).reshape(-1).astype(jnp.int32)
    upsampled = jnp.take(inner_rows, span_of, axis=0)
    mixed_rows = (skip_rows.astype(jnp.float32) + upsampled.astype(jnp.float32)).astype(jnp.bfloat16)
    padded = jnp.pad(mixed_rows.astype(jnp.float32), ((KW - 1, 0), (0, 0)))
    filtered = jnp.zeros((BYTES, DB), jnp.float32)
    for lag_index in range(KW):
        filtered = filtered + conv_kernel[lag_index] * padded[KW - 1 - lag_index:KW - 1 - lag_index + BYTES]
    return (mixed_rows.astype(jnp.float32) + jax.nn.silu(filtered)).astype(jnp.bfloat16)
```

```python
import math

import jax
import jax.numpy as jnp
from jax import lax
from jax.experimental import pallas as pl
from jax.experimental.pallas import tpu as pltpu
from jax.sharding import PartitionSpec as P

HD = 128
CAP = 192
TILE = 16
ROWS = CAP + TILE
NX = 4
NZ = 8
HALF = 384
PIECE = HALF + TILE
QT = 64
HALO = 32
LOG2E = math.log2(math.e)
NEG = -1e30
MIB = 1 << 20
BF = jnp.bfloat16
F32 = jnp.float32


def vmem():
    return pl.BlockSpec(memory_space=pltpu.VMEM)


def anywhere():
    return pl.BlockSpec(memory_space=pl.ANY)


def params(limit=48):
    return pltpu.CompilerParams(vmem_limit_bytes=limit * MIB)


def iota(shape, dim):
    return lax.broadcasted_iota(jnp.int32, shape, dim)


def pool_kernel(len_ref, enc_ref, gain_ref, wk_ref, wv_ref, kv_ref, x_ref, scale_ref, hot, acc, sq):
    step = pl.program_id(0)
    last = pl.num_programs(0) - 1
    byte_rows = enc_ref.shape[0]

    @pl.when(step == 0)
    def _():
        lengths = len_ref[...]
        before = iota((CAP, CAP), 1) < iota((CAP, CAP), 0)
        start = jnp.sum(jnp.where(before, lengths, 0).astype(F32), axis=1, keepdims=True)
        at = iota((CAP, byte_rows), 1).astype(F32)
        hot[...] = jnp.where(at == start, 1.0, 0.0).astype(BF)
        acc[...] = jnp.zeros_like(acc)
        sq[...] = jnp.zeros_like(sq)

    pooled = jnp.dot(hot[...], enc_ref[...], preferred_element_type=F32)
    sq[...] += jnp.sum(pooled * pooled, axis=1, keepdims=True)
    x = (pooled * gain_ref[...]).astype(BF)
    x_ref[...] = x
    acc[:, :HD] += jnp.dot(x, wk_ref[...], preferred_element_type=F32)
    acc[:, HD:] += jnp.dot(x, wv_ref[...], preferred_element_type=F32)

    @pl.when(step == last)
    def _():
        width = x_ref.shape[1] * pl.num_programs(0)
        scale = lax.rsqrt(sq[...] / width + 1e-5)
        scale_ref[...] = jnp.broadcast_to(scale, scale_ref.shape)
        kv_ref[:CAP, :] = (acc[...] * scale).astype(BF)
        count = jnp.sum((len_ref[...] > 0).astype(F32), axis=1, keepdims=True)
        kv_ref[CAP:, :] = jnp.broadcast_to(count, (TILE, 2 * HD)).astype(BF)


def pool(lengths, enc, gain, wk, wv):
    byte_rows, width = enc.shape
    block = 1024
    return pl.pallas_call(
        pool_kernel,
        grid=(width // block,),
        in_specs=[
            pl.BlockSpec((1, CAP), lambda i: (0, 0)),
            pl.BlockSpec((byte_rows, block), lambda i: (0, i)),
            pl.BlockSpec((1, block), lambda i: (0, i)),
            pl.BlockSpec((block, HD), lambda i: (i, 0)),
            pl.BlockSpec((block, HD), lambda i: (i, 0)),
        ],
        out_specs=[
            pl.BlockSpec((ROWS, 2 * HD), lambda i: (0, 0)),
            pl.BlockSpec((CAP, block), lambda i: (0, i)),
            pl.BlockSpec((CAP, HD), lambda i: (0, 0)),
        ],
        out_shape=[
            jax.ShapeDtypeStruct((ROWS, 2 * HD), BF),
            jax.ShapeDtypeStruct((CAP, width), BF),
            jax.ShapeDtypeStruct((CAP, HD), F32),
        ],
        scratch_shapes=[
            pltpu.VMEM((CAP, byte_rows), BF),
            pltpu.VMEM((CAP, 2 * HD), F32),
            pltpu.VMEM((CAP, 1), F32),
        ],
        compiler_params=params(),
        name="pool",
    )(lengths, enc, gain, wk, wv)


def query_kernel(x_ref, wq_ref, scale_ref, q_ref, acc):
    step = pl.program_id(0)

    @pl.when(step == 0)
    def _():
        acc[...] = jnp.zeros_like(acc)

    acc[...] += jnp.dot(x_ref[...], wq_ref[...], preferred_element_type=F32)

    @pl.when(step == pl.num_programs(0) - 1)
    def _():
        scale = scale_ref[:, :1] * (LOG2E * HD**-0.5)
        q_ref[...] = (acc[...] * scale).astype(BF)


def query(x, wq, scale):
    width, out = wq.shape
    block = 1024
    return pl.pallas_call(
        query_kernel,
        grid=(width // block,),
        in_specs=[
            pl.BlockSpec((CAP, block), lambda i: (0, i)),
            pl.BlockSpec((block, out), lambda i: (i, 0)),
            pl.BlockSpec((CAP, HD), lambda i: (0, 0)),
        ],
        out_specs=pl.BlockSpec((CAP, out), lambda i: (0, 0)),
        out_shape=jax.ShapeDtypeStruct((CAP, out), BF),
        scratch_shapes=[pltpu.VMEM((CAP, out), F32)],
        compiler_params=params(),
        cost_estimate=pl.CostEstimate(
            flops=2 * CAP * width * out, bytes_accessed=2 * width * (out + CAP), transcendentals=0
        ),
        name="query",
    )(x, wq, scale)


def compact_kernel(index_ref, *refs):
    blocks, (mine_ref, other_ref) = refs[:8], refs[8:]
    x, core = index_ref[1], index_ref[2]
    shifts = (0, 1, 3, 2)
    order = [
        ((x + NX - shift) % NX) * 2 + (core if side == 0 else 1 - core)
        for side in range(2)
        for shift in shifts
    ]
    counts = [ref[CAP : CAP + TILE, :].astype(F32)[:1, :] for ref in blocks]
    lane = iota((1, CAP), 1).astype(F32)
    targets = []
    for i in range(8):
        first = jnp.zeros((1, 2 * HD), F32)
        for k in range(8):
            if k != i:
                first += jnp.where(order[k] < order[i], counts[k], 0.0)
        targets.append(jnp.where(lane < counts[i][:, :CAP], first[:, :CAP] + lane, -1.0))
    sub = iota((TILE, 2 * HD), 0)
    table = jnp.zeros((TILE, 2 * HD), F32)
    for i in range(8):
        table += jnp.where(sub == order[i], counts[i], 0.0)
    for half, out in ((core, mine_ref), (1 - core, other_ref)):
        row = (iota((HALF, CAP), 0) + half * HALF).astype(F32)
        total = jnp.zeros((HALF, 2 * HD), F32)
        for i in range(8):
            hot = jnp.where(row == targets[i], 1.0, 0.0).astype(BF)
            total += jnp.dot(hot, blocks[i][:CAP, :], preferred_element_type=F32)
        out[:HALF, :] = total.astype(BF)
        out[HALF:, :] = table.astype(BF)


def compact(index, blocks):
    return pl.pallas_call(
        compact_kernel,
        in_specs=[pl.BlockSpec(memory_space=pltpu.SMEM)] + [vmem()] * 8,
        out_specs=[vmem()] * 2,
        out_shape=[jax.ShapeDtypeStruct((PIECE, 2 * HD), BF)] * 2,
        compiler_params=params(),
        name="compact",
    )(index, *blocks)


def attend_kernel(index_ref, len_ref, q_ref, wout_ref, *refs):
    n_in = 18
    pieces, outs = refs[:n_in], refs[n_in : n_in + 4]
    kv, scores, sems = refs[n_in + 4 :]
    z, x, core, y = index_ref[0], index_ref[1], index_ref[2], index_ref[3]
    plan = []
    for k, (plane, needed) in enumerate(
        [(z, z >= 0)]
        + [(z - s, z >= s) for s in (1, 2, 3)]
        + [(z + s - NZ, z >= NZ - s) for s in (1, 2, 3)]
    ):
        for side in range(2):
            plan.append((pieces[2 * k + side], side, plane, needed, 0))
    for side in range(2):
        plan.append((pieces[14 + side], side, z - 4, z >= 4, 0))
        plan.append((pieces[16 + side], side, z - 4, z >= 4, CAP))
    copies = []
    for k, (ref, side, plane, needed, first) in enumerate(plan):
        half = core if side == 0 else 1 - core
        slot = jnp.maximum(plane, 0) * 2 + half
        copy = pltpu.make_async_copy(
            ref, kv.at[slot, pl.ds(first, ref.shape[0])], sems.at[k]
        )
        copies.append((copy, needed))
        pl.when(needed)(copy.start)
    for out in outs:
        out[...] = jnp.zeros_like(out)
    count = jnp.sum((len_ref[...] > 0).astype(jnp.int32))
    for copy, needed in copies:
        pl.when(needed)(copy.wait)
    own = x * 2 + core
    key_lane = iota((1, HALF), 1).astype(F32)
    table_own = kv[2 * z, HALF:, :].astype(F32)
    first_own = jnp.sum(
        jnp.where(iota((TILE, 2 * HD), 0) < own, table_own, 0.0), axis=0, keepdims=True
    )[:, :1]

    def per_tile(tile, _):
        slots = pl.ds(pl.multiple_of(tile * QT, QT), QT)
        q = jnp.concatenate([q_ref[slots, h * HD : (h + 1) * HD] for h in range(4)], axis=0)

        def top(run, s):
            for k in range(HALF // HD):
                run = jnp.maximum(run, s[:, k * HD : (k + 1) * HD])
            return run

        def first_pass(b, run):
            s = lax.dot_general(
                q, kv[b, :HALF, :HD], (((1,), (1,)), ((), ())), preferred_element_type=F32
            )
            live = jnp.sum(kv[b, HALF:, :].astype(F32), axis=0, keepdims=True)[:, :1]
            pos = key_lane + ((b % 2) * HALF).astype(F32)
            s = s + jnp.where(pos < live, 0.0, NEG)
            scores[b] = s
            return top(run, s)

        run = lax.fori_loop(0, 2 * z, first_pass, jnp.full((4 * QT, HD), NEG, F32))
        query_pos = first_own + (tile * QT + iota((4 * QT, 1), 0) % QT).astype(F32)
        for h in range(2):
            b = 2 * z + h
            s = lax.dot_general(
                q, kv[b, :HALF, :HD], (((1,), (1,)), ((), ())), preferred_element_type=F32
            )
            s = jnp.where(key_lane + float(h * HALF) <= query_pos, s, NEG)
            scores[b] = s
            run = top(run, s)
        m = jnp.max(run, axis=1, keepdims=True)

        def second_pass(b, carry):
            o, l = carry
            p = jnp.exp2(scores[b] - m)
            for k in range(HALF // HD):
                l = l + p[:, k * HD : (k + 1) * HD]
            o = o + jnp.dot(p.astype(BF), kv[b, :HALF, HD:], preferred_element_type=F32)
            return o, l

        zero = jnp.zeros((4 * QT, HD), F32)
        o, l = lax.fori_loop(0, 2 * z + 2, second_pass, (zero, zero))
        a = (o / jnp.sum(l, axis=1, keepdims=True)).astype(BF)
        for k in range(4):
            cols = pl.ds(pl.multiple_of(((y + k) % 4) * 256, 256), 256)
            part = jnp.zeros((QT, 256), F32)
            for h in range(4):
                part += jnp.dot(
                    a[h * QT : (h + 1) * QT, :],
                    wout_ref[h * HD : (h + 1) * HD, cols],
                    preferred_element_type=F32,
                )
            outs[k][slots, :] = part.astype(BF)
        return 0

    lax.fori_loop(0, (count + QT - 1) // QT, per_tile, 0)


def attend(index, lengths, q, wout, pieces):
    return pl.pallas_call(
        attend_kernel,
        in_specs=[pl.BlockSpec(memory_space=pltpu.SMEM)] + [vmem()] * 3 + [anywhere()] * len(pieces),
        out_specs=[vmem()] * 4,
        out_shape=[jax.ShapeDtypeStruct((CAP, 256), BF)] * 4,
        scratch_shapes=[
            pltpu.VMEM((2 * NZ, PIECE, 2 * HD), BF),
            pltpu.VMEM((2 * NZ, 4 * QT, HALF), F32),
            pltpu.SemaphoreType.DMA((len(pieces),)),
        ],
        compiler_params=params(),
        name="attend",
    )(index, lengths, q, wout, *pieces)


def attend_any(kv, q, lengths, wout, y):
    everyone = lax.all_gather(kv, "seq", axis=0)
    device = lax.axis_index("seq")
    queries = q.reshape(CAP, 4, HD)
    slot = jnp.arange(CAP, dtype=jnp.int32)

    def step(carry, part):
        top, total, weighted = carry
        block, source = part
        keys, values = block[:CAP, :HD], block[:CAP, HD:]
        live = block[CAP, 0].astype(jnp.int32)
        s = jnp.einsum("wgd,rd->wgr", queries, keys, preferred_element_type=F32)
        later = (source == device) & (slot[None, :] > slot[:, None])
        allowed = ((slot < live)[None, :] & (source <= device) & ~later)[:, None, :]
        s = jnp.where(allowed, s, NEG)
        new = jnp.maximum(top, jnp.max(s, axis=2))
        factor = jnp.exp2(top - new)
        w = jnp.where(allowed, jnp.exp2(s - new[..., None]), 0.0)
        total = total * factor + jnp.sum(w, axis=2)
        weighted = weighted * factor[..., None] + jnp.einsum(
            "wgr,rd->wgd", w.astype(BF), values, preferred_element_type=F32
        )
        return (new, total, weighted), None

    start = (
        jnp.full((CAP, 4), NEG, F32),
        jnp.zeros((CAP, 4), F32),
        jnp.zeros((CAP, 4, HD), F32),
    )
    sources = jnp.arange(everyone.shape[0], dtype=jnp.int32)
    (_, total, weighted), _ = lax.scan(step, start, (everyone, sources))
    a = (weighted / total[..., None]).reshape(CAP, 4 * HD).astype(BF)
    part = jnp.dot(a, wout, preferred_element_type=F32).astype(BF)
    return [lax.dynamic_slice_in_dim(part, ((y + k) % 4) * 256, 256, 1) for k in range(4)]


def mix_kernel(len_ref, skip_ref, p0, p1, p2, p3, mixed_ref, tail_ref):
    byte_rows = skip_ref.shape[0]
    lengths = len_ref[...].astype(F32)
    inner = p0[...].astype(F32) + p1[...].astype(F32) + p2[...].astype(F32) + p3[...].astype(F32)
    i, j = iota((CAP, CAP), 0), iota((CAP, CAP), 1)
    column = jnp.sum(jnp.where(i == j, lengths, 0.0), axis=1, keepdims=True)
    start = jnp.sum(jnp.where(i < j, column, 0.0), axis=0, keepdims=True)
    at = iota((byte_rows, CAP), 0).astype(F32)
    hot = jnp.where((at >= start) & (at < start + lengths), 1.0, 0.0).astype(BF)
    up = jnp.dot(hot, inner.astype(BF), preferred_element_type=F32)
    mixed = (skip_ref[...].astype(F32) + up).astype(BF)
    mixed_ref[...] = mixed
    tail_ref[...] = mixed[byte_rows - HALO :, :]


def mix(lengths, skip, parts):
    return pl.pallas_call(
        mix_kernel,
        in_specs=[vmem()] * 6,
        out_specs=[vmem()] * 2,
        out_shape=[
            jax.ShapeDtypeStruct(skip.shape, BF),
            jax.ShapeDtypeStruct((HALO, skip.shape[1]), BF),
        ],
        compiler_params=params(),
        name="mix",
    )(lengths, skip, *parts)


def conv_kernel_body(mixed_ref, rim_ref, taps_ref, out_ref, ext):
    byte_rows = mixed_ref.shape[0]
    ext[:HALO, :] = rim_ref[...].astype(F32)
    ext[HALO:, :] = mixed_ref[...].astype(F32)
    block = 64

    def per_block(i, _):
        first = pl.multiple_of(i * block, block)
        window = ext[pl.ds(first, block + HALO), :]
        total = jnp.zeros((block, mixed_ref.shape[1]), F32)
        for lag in range(taps_ref.shape[0]):
            total += taps_ref[lag : lag + 1, :] * window[HALO - lag : HALO - lag + block, :]
        here = window[HALO:, :]
        out_ref[pl.ds(first, block), :] = (here + total / (1.0 + jnp.exp(-total))).astype(BF)
        return 0

    lax.fori_loop(0, byte_rows // block, per_block, 0)


def convolve(mixed, rim, taps):
    return pl.pallas_call(
        conv_kernel_body,
        in_specs=[vmem()] * 3,
        out_specs=vmem(),
        out_shape=jax.ShapeDtypeStruct(mixed.shape, BF),
        scratch_shapes=[pltpu.VMEM((HALO + mixed.shape[0], mixed.shape[1]), F32)],
        compiler_params=params(),
        name="convolve",
    )(mixed, rim, taps)


def seq_permute(value, move):
    pairs = []
    for z in range(NZ):
        for x in range(NX):
            for core in range(2):
                tz, tx, tc = move(z, x, core)
                target = ((tz % NZ) * NX + tx % NX) * 2 + tc
                pairs.append(((z * NX + x) * 2 + core, target))
    return lax.ppermute(value, "seq", pairs)


def along_x(value, steps):
    return seq_permute(value, lambda z, x, c: (z, x + steps, c))


def along_z(value, steps):
    return seq_permute(value, lambda z, x, c: (z + steps, x, c))


def swap(value):
    return seq_permute(value, lambda z, x, c: (z, x, 1 - c))


def per_device(enc, span_len, skip, gain, wq, wk, wv, wout, taps):
    seq = lax.axis_index("seq")
    y = lax.axis_index("section")
    index = jnp.stack([seq // (2 * NX), (seq // 2) % NX, seq % 2, y]).astype(jnp.int32)
    kv, x, scale = pool(span_len, enc, gain.reshape(1, -1), wk, wv)
    column = [kv, along_x(kv, 1), along_x(kv, -1), along_x(kv, 2)]
    q = query(x, wq, scale)
    mine, other = compact(index, column + [swap(v) for v in column])
    right, left = [mine], [mine]
    for _ in range(3):
        right.append(along_z(right[-1], 1))
        left.append(along_z(left[-1], -1))
    far_low = along_z(right[3][:CAP], 1)
    far_high = along_z(left[3][CAP:], -1)
    got = right[1:] + left[1:] + [far_low, far_high]
    pieces = [mine, other]
    for piece in got:
        pieces += [piece, swap(piece)]
    tables = [piece[-TILE:, 0].astype(F32) for piece in [mine] + got[:6] + [far_high]]
    most = jnp.max(jnp.stack([jnp.sum(table) for table in tables]))
    parts = lax.cond(
        most > 2 * HALF,
        lambda: attend_any(kv, q, span_len, wout, y),
        lambda: list(attend(index, span_len, q, wout, pieces)),
    )
    sent = [
        lax.ppermute(parts[k], "section", [(i, (i + k) % 4) for i in range(4)]) for k in (1, 2, 3)
    ]
    mixed, tail = mix(span_len, skip, [parts[0]] + sent)
    rim = lax.ppermute(tail, "seq", [(i, i + 1) for i in range(2 * NX * NZ - 1)])
    return convolve(mixed, rim, taps)


def solution(mesh):
    return jax.shard_map(
        per_device,
        mesh=mesh,
        in_specs=(
            P("seq", None),
            P("seq", None),
            P("seq", "section"),
            P(),
            P(None, "section"),
            P(None, "section"),
            P(None, "section"),
            P("section", None),
            P(None, "section"),
        ),
        out_specs=P("seq", "section"),
        check_vma=False,
    )
```

```python
import math

import jax
import jax.numpy as jnp
from jax import lax
from jax.experimental import pallas as pl
from jax.experimental.pallas import tpu as pltpu
from jax.sharding import PartitionSpec as P

HD = 128
CAP = 192
TILE = 16
ROWS = CAP + TILE
NX = 4
NZ = 8
HALF = 384
UPPER = HALF + TILE
PIECE = UPPER + HALF
QT = 96
KEYS = 512
POOL_STEPS = 4
FULL = 63
QUERY_LIMIT = 62
HALO = 32
LOG2E = math.log2(math.e)
NEG = -1e30
MIB = 1 << 20
BF = jnp.bfloat16
F32 = jnp.float32


def vmem():
    return pl.BlockSpec(memory_space=pltpu.VMEM)


def anywhere():
    return pl.BlockSpec(memory_space=pl.ANY)


def params(limit=48):
    return pltpu.CompilerParams(vmem_limit_bytes=limit * MIB)


def iota(shape, dim):
    return lax.broadcasted_iota(jnp.int32, shape, dim)


def pool_kernel(len_hbm, gain_hbm, enc_hbm, wk_hbm, wv_hbm, kv_ref, x_hbm, scale_ref, lengths, gain, enc, wkv, x, sems):
    byte_rows, width = enc.shape
    block = width // POOL_STEPS
    small = [
        pltpu.make_async_copy(len_hbm, lengths, sems.at[0]),
        pltpu.make_async_copy(gain_hbm, gain, sems.at[1]),
    ]
    for copy in small:
        copy.start()
    copies = []
    for step in range(POOL_STEPS):
        part = pl.ds(step * block, block)
        at = 2 + 3 * step
        group = [
            pltpu.make_async_copy(enc_hbm.at[:, part], enc.at[:, part], sems.at[at]),
            pltpu.make_async_copy(wk_hbm.at[part], wkv.at[part, pl.ds(0, HD)], sems.at[at + 1]),
            pltpu.make_async_copy(wv_hbm.at[part], wkv.at[part, pl.ds(HD, HD)], sems.at[at + 2]),
        ]
        for copy in group:
            copy.start()
        copies.append(group)
    for copy in small:
        copy.wait()
    before = iota((CAP, CAP), 1) < iota((CAP, CAP), 0)
    start = jnp.sum(jnp.where(before, lengths[...], 0).astype(F32), axis=1, keepdims=True)
    hot = jnp.where(iota((CAP, byte_rows), 1).astype(F32) == start, 1.0, 0.0).astype(BF)
    total = jnp.zeros((CAP, 2 * HD), F32)
    squares = jnp.zeros((CAP, HD), F32)
    leaving = []
    held = None
    for step in range(POOL_STEPS + 1):
        if step < POOL_STEPS:
            for copy in copies[step]:
                copy.wait()
        if held is not None:
            last = slice((step - 1) * block, step * block)
            total += jnp.dot(held, wkv[last, :], preferred_element_type=F32)
        if step < POOL_STEPS:
            part = slice(step * block, (step + 1) * block)
            pooled = jnp.dot(hot, enc[:, part], preferred_element_type=F32)
            for k in range(block // HD):
                piece = pooled[:, k * HD : (k + 1) * HD]
                squares += piece * piece
            held = (pooled * gain[:, part]).astype(BF)
            x[:, part] = held
            leaving.append(
                pltpu.make_async_copy(
                    x.at[:, pl.ds(step * block, block)],
                    x_hbm.at[:, pl.ds(step * block, block)],
                    sems.at[2 + 3 * POOL_STEPS + step],
                )
            )
            leaving[-1].start()
    scale = lax.rsqrt(jnp.sum(squares, axis=1, keepdims=True) / width + 1e-5)
    scale_ref[...] = jnp.broadcast_to(scale, scale_ref.shape)
    kv_ref[:CAP, :] = (total * scale).astype(BF)
    count = jnp.sum((lengths[...] > 0).astype(F32), axis=1, keepdims=True)
    kv_ref[CAP:, :] = jnp.broadcast_to(count, (TILE, 2 * HD)).astype(BF)
    for copy in leaving:
        copy.wait()


def pool(lengths, enc, gain, wk, wv):
    byte_rows, width = enc.shape
    return pl.pallas_call(
        pool_kernel,
        in_specs=[anywhere()] * 5,
        out_specs=[vmem(), anywhere(), vmem()],
        out_shape=[
            jax.ShapeDtypeStruct((ROWS, 2 * HD), BF),
            jax.ShapeDtypeStruct((CAP, width), BF),
            jax.ShapeDtypeStruct((CAP, HD), F32),
        ],
        scratch_shapes=[
            pltpu.VMEM(lengths.shape, jnp.int32),
            pltpu.VMEM(gain.shape, F32),
            pltpu.VMEM((byte_rows, width), BF),
            pltpu.VMEM((width, 2 * HD), BF),
            pltpu.VMEM((CAP, width), BF),
            pltpu.SemaphoreType.DMA((4 * POOL_STEPS + 2,)),
        ],
        compiler_params=params(FULL),
        cost_estimate=pl.CostEstimate(
            flops=2 * CAP * width * (byte_rows + 2 * HD),
            bytes_accessed=2 * width * (byte_rows + CAP + 2 * HD),
            transcendentals=0,
        ),
        name="pool",
    )(lengths, gain, enc, wk, wv)


def query_kernel(x_hbm, scale_ref, wq_hbm, q_ref, x, wq, sems):
    width = wq.shape[0]
    block = width // POOL_STEPS
    copies = []
    for step in range(POOL_STEPS):
        part = pl.ds(step * block, block)
        copies.append(
            [
                pltpu.make_async_copy(wq_hbm.at[part], wq.at[part], sems.at[2 * step]),
                pltpu.make_async_copy(x_hbm.at[:, part], x.at[:, part], sems.at[2 * step + 1]),
            ]
        )
        for copy in copies[-1]:
            copy.start()
    total = jnp.zeros(q_ref.shape, F32)
    for step in range(POOL_STEPS):
        for copy in copies[step]:
            copy.wait()
        part = slice(step * block, (step + 1) * block)
        total += jnp.dot(x[:, part], wq[part, :], preferred_element_type=F32)
    q_ref[...] = (total * (scale_ref[:, :1] * (LOG2E * HD**-0.5))).astype(BF)


def query(x, wq, scale):
    width, out = wq.shape
    return pl.pallas_call(
        query_kernel,
        in_specs=[anywhere(), vmem(), anywhere()],
        out_specs=vmem(),
        out_shape=jax.ShapeDtypeStruct((CAP, out), BF),
        scratch_shapes=[
            pltpu.VMEM((CAP, width), BF),
            pltpu.VMEM((width, out), BF),
            pltpu.SemaphoreType.DMA((2 * POOL_STEPS,)),
        ],
        compiler_params=params(QUERY_LIMIT),
        cost_estimate=pl.CostEstimate(
            flops=2 * CAP * width * out, bytes_accessed=2 * width * (out + CAP), transcendentals=0
        ),
        name="query",
    )(x, scale, wq)


def compact_kernel(index_ref, *refs):
    blocks, out_ref = refs[:8], refs[8]
    x, core = index_ref[1], index_ref[2]
    shifts = (0, 1, 3, 2)
    order = [
        ((x + NX - shift) % NX) * 2 + (core if side == 0 else 1 - core)
        for side in range(2)
        for shift in shifts
    ]
    counts = [ref[CAP : CAP + TILE, :].astype(F32)[:1, :] for ref in blocks]
    lane = iota((1, CAP), 1).astype(F32)
    targets = []
    for i in range(8):
        first = jnp.zeros((1, 2 * HD), F32)
        for k in range(8):
            if k != i:
                first += jnp.where(order[k] < order[i], counts[k], 0.0)
        targets.append(jnp.where(lane < counts[i][:, :CAP], first[:, :CAP] + lane, -1.0))
    sub = iota((TILE, 2 * HD), 0)
    table = jnp.zeros((TILE, 2 * HD), F32)
    for i in range(8):
        table += jnp.where(sub == order[i], counts[i], 0.0)
    out_ref[HALF:UPPER, :] = table.astype(BF)
    for half in range(2):
        row = (iota((HALF, CAP), 0) + half * HALF).astype(F32)
        total = jnp.zeros((HALF, 2 * HD), F32)
        for i in range(8):
            hot = jnp.where(row == targets[i], 1.0, 0.0).astype(BF)
            total += jnp.dot(hot, blocks[i][:CAP, :], preferred_element_type=F32)
        out_ref[half * UPPER : half * UPPER + HALF, :] = total.astype(BF)


def compact(index, blocks):
    return pl.pallas_call(
        compact_kernel,
        in_specs=[pl.BlockSpec(memory_space=pltpu.SMEM)] + [vmem()] * 8,
        out_specs=vmem(),
        out_shape=jax.ShapeDtypeStruct((PIECE, 2 * HD), BF),
        compiler_params=params(),
        name="compact",
    )(index, *blocks)


def attend_kernel(index_ref, len_ref, q_ref, wout_ref, *refs):
    n_in = 9
    pieces, outs, flag_ref = refs[:n_in], refs[n_in : n_in + 4], refs[n_in + 4]
    keys, values, scores, top, acc, lsum = refs[n_in + 5 :]
    z, x, core, y = index_ref[0], index_ref[1], index_ref[2], index_ref[3]
    own = x * 2 + core
    for out in outs:
        out[...] = jnp.zeros_like(out)

    own_piece, came, swapped = pieces[0], pieces[1:5], pieces[5:9]
    upward, downward = (came, swapped), (swapped, came)

    def plain(refs):
        return [[(ref, 0, 0), (ref, UPPER, HALF)] for ref in refs]

    planes = [(8 - s, plain([downward[c][s - 1] for c in range(2)])) for s in (1, 2, 3)]
    planes.append((4, [[(upward[c][3], 0, 0), (downward[c][3], TILE, HALF)] for c in range(2)]))
    planes += [(s, plain([upward[c][s - 1] for c in range(2)])) for s in (3, 2, 1)]
    planes.append((0, plain([own_piece, own_piece])))

    def table(back, halves):
        found = [ref[HALF:UPPER, :HD].astype(F32) for (ref, _, _), _ in halves]
        return jnp.where(core == 0, found[0], found[1]) if back else found[0]

    def single(value):
        return jnp.max(jnp.sum(value, axis=0, keepdims=True)).astype(jnp.int32)

    lives = [single(table(back, halves)) for back, halves in planes]
    most = lives[0]
    for live in lives[1:]:
        most = jnp.maximum(most, live)
    flag_ref[0] = (most > 2 * HALF).astype(jnp.int32)
    own_table = table(*planes[-1])
    row = iota((TILE, HD), 0)
    before = single(jnp.where(row < own, own_table, 0.0))
    count = single(jnp.where(row == own, own_table, 0.0))

    first = jnp.int32(0)
    half_row = iota((HALF, HD), 0)
    for (back, halves), live in zip(planes, lives):
        here = jnp.minimum(live, 2 * HALF)
        for c in range(2 if back else 1):
            wanted = (z >= back) & (core == c) if back else z >= 0

            @pl.when(wanted)
            def _(moves=halves[c], here=here, first=first):
                for ref, low, to_row in moves:
                    to = pl.ds(pl.multiple_of(first + to_row, TILE), HALF)
                    keys[to, :HD] = ref[low : low + HALF, :HD]
                    values[to, :] = ref[low : low + HALF, HD:]
                    dead = jnp.where(half_row + to_row < here, 0.0, NEG)
                    keys[to, HD:] = dead.astype(BF)

        if back:
            first = first + jnp.where(z >= back, (here + TILE - 1) // TILE * TILE, 0)
    end = pl.ds(pl.multiple_of(first + 2 * HALF, TILE), KEYS)
    keys[end, :] = jnp.zeros((KEYS, 2 * HD), BF)
    values[end, :] = jnp.zeros((KEYS, HD), BF)
    free = first // KEYS
    chunks = (first + before + count + KEYS - 1) // KEYS
    ones = jnp.where(iota((4 * QT, HD), 1) == 0, 1.0, 0.0).astype(BF)

    def per_tile(tile, _):
        slots = pl.ds(pl.multiple_of(tile * QT, QT), QT)
        q = jnp.concatenate([q_ref[slots, h * HD : (h + 1) * HD] for h in range(4)], axis=0)
        q = jnp.concatenate([q, ones], axis=1)
        top[...] = jnp.full(top.shape, NEG, F32)
        acc[...] = jnp.zeros_like(acc)
        lsum[...] = jnp.zeros_like(lsum)

        def score(c):
            rows = pl.ds(pl.multiple_of(c * KEYS, KEYS), KEYS)
            return lax.dot_general(
                q, keys[rows, :], (((1,), (1,)), ((), ())), preferred_element_type=F32
            )

        def keep(c, s):
            scores[c] = s
            best = top[...]
            for k in range(KEYS // HD):
                best = jnp.maximum(best, s[:, k * HD : (k + 1) * HD])
            top[...] = best

        def open_chunk(c, _):
            keep(c, score(c))
            return 0

        query_pos = first + before + tile * QT + iota((4 * QT, 1), 0) % QT

        def masked_chunk(c, _):
            allowed = c * KEYS + iota((4 * QT, KEYS), 1) <= query_pos
            keep(c, jnp.where(allowed, score(c), NEG))
            return 0

        lax.fori_loop(0, free, open_chunk, 0)
        lax.fori_loop(free, chunks, masked_chunk, 0)
        top[...] = jnp.broadcast_to(jnp.max(top[...], axis=1, keepdims=True), top.shape)

        def weigh(c, _):
            best = top[...]
            parts = [
                jnp.exp2(scores[c, :, k * HD : (k + 1) * HD] - best) for k in range(KEYS // HD)
            ]
            total = parts[0]
            for part in parts[1:]:
                total = total + part
            lsum[...] += total
            p = jnp.concatenate([part.astype(BF) for part in parts], axis=1)
            rows = pl.ds(pl.multiple_of(c * KEYS, KEYS), KEYS)
            acc[...] += jnp.dot(p, values[rows, :], preferred_element_type=F32)
            return 0

        lax.fori_loop(0, chunks, weigh, 0)
        a = (acc[...] / jnp.sum(lsum[...], axis=1, keepdims=True)).astype(BF)
        a = jnp.concatenate([a[h * QT : (h + 1) * QT, :] for h in range(4)], axis=1)
        for k in range(4):
            cols = pl.ds(pl.multiple_of(((y + k) % 4) * 256, 256), 256)
            outs[k][slots, :] = jnp.dot(
                a, wout_ref[:, cols], preferred_element_type=F32
            ).astype(BF)
        return 0

    lax.fori_loop(0, (count + QT - 1) // QT, per_tile, 0)


def attend(index, lengths, q, wout, pieces):
    most = 2 * NZ * HALF + KEYS
    *parts, flag = pl.pallas_call(
        attend_kernel,
        in_specs=[pl.BlockSpec(memory_space=pltpu.SMEM)] + [vmem()] * (3 + len(pieces)),
        out_specs=[vmem()] * 4 + [pl.BlockSpec(memory_space=pltpu.SMEM)],
        out_shape=[jax.ShapeDtypeStruct((CAP, 256), BF)] * 4
        + [jax.ShapeDtypeStruct((1,), jnp.int32)],
        scratch_shapes=[
            pltpu.VMEM((most, 2 * HD), BF),
            pltpu.VMEM((most, HD), BF),
            pltpu.VMEM((most // KEYS, 4 * QT, KEYS), F32),
            pltpu.VMEM((4 * QT, HD), F32),
            pltpu.VMEM((4 * QT, HD), F32),
            pltpu.VMEM((4 * QT, HD), F32),
        ],
        compiler_params=params(),
        name="attend",
    )(index, lengths, q, wout, *pieces)
    return parts, flag[0]


def attend_any(kv, q, lengths, wout, y):
    everyone = lax.all_gather(kv, "seq", axis=0)
    device = lax.axis_index("seq")
    queries = q.reshape(CAP, 4, HD)
    slot = jnp.arange(CAP, dtype=jnp.int32)

    def step(carry, part):
        top, total, weighted = carry
        block, source = part
        keys, values = block[:CAP, :HD], block[:CAP, HD:]
        live = block[CAP, 0].astype(jnp.int32)
        s = jnp.einsum("wgd,rd->wgr", queries, keys, preferred_element_type=F32)
        later = (source == device) & (slot[None, :] > slot[:, None])
        allowed = ((slot < live)[None, :] & (source <= device) & ~later)[:, None, :]
        s = jnp.where(allowed, s, NEG)
        new = jnp.maximum(top, jnp.max(s, axis=2))
        factor = jnp.exp2(top - new)
        w = jnp.where(allowed, jnp.exp2(s - new[..., None]), 0.0)
        total = total * factor + jnp.sum(w, axis=2)
        weighted = weighted * factor[..., None] + jnp.einsum(
            "wgr,rd->wgd", w.astype(BF), values, preferred_element_type=F32
        )
        return (new, total, weighted), None

    start = (
        jnp.full((CAP, 4), NEG, F32),
        jnp.zeros((CAP, 4), F32),
        jnp.zeros((CAP, 4, HD), F32),
    )
    sources = jnp.arange(everyone.shape[0], dtype=jnp.int32)
    (_, total, weighted), _ = lax.scan(step, start, (everyone, sources))
    a = (weighted / total[..., None]).reshape(CAP, 4 * HD).astype(BF)
    part = jnp.dot(a, wout, preferred_element_type=F32).astype(BF)
    return [lax.dynamic_slice_in_dim(part, ((y + k) % 4) * 256, 256, 1) for k in range(4)]


def mix_kernel(len_ref, skip_ref, p0, p1, p2, p3, mixed_ref, tail_ref):
    byte_rows = skip_ref.shape[0]
    lengths = len_ref[...].astype(F32)
    inner = p0[...].astype(F32) + p1[...].astype(F32) + p2[...].astype(F32) + p3[...].astype(F32)
    i, j = iota((CAP, CAP), 0), iota((CAP, CAP), 1)
    column = jnp.sum(jnp.where(i == j, lengths, 0.0), axis=1, keepdims=True)
    start = jnp.sum(jnp.where(i < j, column, 0.0), axis=0, keepdims=True)
    at = iota((byte_rows, CAP), 0).astype(F32)
    hot = jnp.where((at >= start) & (at < start + lengths), 1.0, 0.0).astype(BF)
    up = jnp.dot(hot, inner.astype(BF), preferred_element_type=F32)
    mixed = (skip_ref[...].astype(F32) + up).astype(BF)
    mixed_ref[...] = mixed
    tail_ref[...] = mixed[byte_rows - HALO :, :]


def mix(lengths, skip, parts):
    return pl.pallas_call(
        mix_kernel,
        in_specs=[vmem()] * 6,
        out_specs=[vmem()] * 2,
        out_shape=[
            jax.ShapeDtypeStruct(skip.shape, BF),
            jax.ShapeDtypeStruct((HALO, skip.shape[1]), BF),
        ],
        compiler_params=params(),
        name="mix",
    )(lengths, skip, *parts)


def filtered(window, taps):
    rows = window.shape[0] - HALO
    total = jnp.zeros((rows, window.shape[1]), F32)
    lags = taps.shape[0]
    for r in range(8):
        moved = window[8 - r : rows + HALO - r, :]
        for lag in range(r, lags, 8):
            low = HALO - 8 - (lag - r)
            total += taps[lag : lag + 1, :] * moved[low : low + rows, :]
    return (window[HALO:, :] + total / (1.0 + jnp.exp(-total))).astype(BF)


def conv_kernel(mixed_ref, taps_ref, out_ref, ext):
    byte_rows, channels = mixed_ref.shape
    ext[:HALO, :] = jnp.zeros((HALO, channels), F32)
    ext[HALO:, :] = mixed_ref[...].astype(F32)
    block = 64

    def per_block(i, _):
        first = pl.multiple_of(i * block, block)
        for low in range(0, channels, 128):
            part = slice(low, low + 128)
            window = ext[pl.ds(first, block + HALO), part]
            out_ref[pl.ds(first, block), part] = filtered(window, taps_ref[:, part])
        return 0

    lax.fori_loop(0, byte_rows // block, per_block, 0)


def rim_kernel(given_hbm, rim_ref, mixed_ref, taps_ref, out_hbm, rows, sem):
    del given_hbm
    for low in range(0, mixed_ref.shape[1], 128):
        part = slice(low, low + 128)
        window = jnp.concatenate([rim_ref[:, part], mixed_ref[:HALO, part]], axis=0).astype(F32)
        rows[:, part] = filtered(window, taps_ref[:, part])
    copy = pltpu.make_async_copy(rows, out_hbm.at[pl.ds(0, HALO)], sem)
    copy.start()
    copy.wait()


def convolve(mixed, taps):
    return pl.pallas_call(
        conv_kernel,
        in_specs=[vmem()] * 2,
        out_specs=vmem(),
        out_shape=jax.ShapeDtypeStruct(mixed.shape, BF),
        scratch_shapes=[pltpu.VMEM((HALO + mixed.shape[0], mixed.shape[1]), F32)],
        compiler_params=params(),
        cost_estimate=pl.CostEstimate(
            flops=2 * mixed.size * taps.shape[0], bytes_accessed=16 * mixed.size, transcendentals=0
        ),
        name="convolve",
    )(mixed, taps)


def first_rows(given, rim, mixed, taps):
    return pl.pallas_call(
        rim_kernel,
        in_specs=[anywhere()] + [vmem()] * 3,
        out_specs=anywhere(),
        out_shape=jax.ShapeDtypeStruct(given.shape, BF),
        input_output_aliases={0: 0},
        scratch_shapes=[pltpu.VMEM((HALO, mixed.shape[1]), BF), pltpu.SemaphoreType.DMA],
        compiler_params=params(),
        name="first_rows",
    )(given, rim, mixed, taps)


def seq_permute(value, move):
    pairs = []
    for z in range(NZ):
        for x in range(NX):
            for core in range(2):
                tz, tx, tc = move(z, x, core)
                target = ((tz % NZ) * NX + tx % NX) * 2 + tc
                pairs.append(((z * NX + x) * 2 + core, target))
    return lax.ppermute(value, "seq", pairs)


def along_x(value, steps):
    return seq_permute(value, lambda z, x, c: (z, x + steps, c))


def round_z(value):
    return seq_permute(value, lambda z, x, c: (z + 1 - 2 * c, x, c))


def swap(value):
    return seq_permute(value, lambda z, x, c: (z, x, 1 - c))


def per_device(enc, span_len, skip, gain, wq, wk, wv, wout, taps):
    seq = lax.axis_index("seq")
    y = lax.axis_index("section")
    index = jnp.stack([seq // (2 * NX), (seq // 2) % NX, seq % 2, y]).astype(jnp.int32)
    kv, x, scale = pool(span_len, enc, gain.reshape(1, -1), wk, wv)
    there = [along_x(kv, 1), along_x(kv, -1), along_x(kv, 2)]
    there, q = lax.optimization_barrier((there, query(x, wq, scale)))
    column = [kv] + there
    plane = compact(index, column + [swap(v) for v in column])
    came = [round_z(plane)]
    came.append(round_z(came[-1]))
    came.append(round_z(came[-1]))
    came.append(round_z(lax.dynamic_slice_in_dim(came[-1], (seq % 2) * HALF, UPPER, 0)))
    pieces = [plane] + came + [swap(piece) for piece in came]
    parts, crowded = attend(index, span_len, q, wout, pieces)
    parts = lax.cond(
        crowded > 0, lambda _: attend_any(kv, q, span_len, wout, y), lambda given: given, parts
    )
    sent = [
        lax.ppermute(parts[k], "section", [(i, (i + k) % 4) for i in range(4)]) for k in (1, 2, 3)
    ]
    mixed, tail = mix(span_len, skip, [parts[0]] + sent)
    rim = lax.ppermute(tail, "seq", [(i, i + 1) for i in range(2 * NX * NZ - 1)])
    return first_rows(convolve(mixed, taps), rim, mixed, taps)


def solution(mesh):
    return jax.shard_map(
        per_device,
        mesh=mesh,
        in_specs=(
            P("seq", None),
            P("seq", None),
            P("seq", "section"),
            P(),
            P(None, "section"),
            P(None, "section"),
            P(None, "section"),
            P("section", None),
            P(None, "section"),
        ),
        out_specs=P("seq", "section"),
        check_vma=False,
    )
```

```python
import math

import jax
import jax.numpy as jnp
from jax import lax
from jax.experimental import pallas as pl
from jax.experimental.pallas import tpu as pltpu
from jax.sharding import PartitionSpec as P

HD = 128
CAP = 192
TILE = 16
ROWS = CAP + TILE
NX = 4
NZ = 8
HALF = 384
UPPER = HALF + TILE
PIECE = UPPER + HALF
QT = 96
KEYS = 512
POOL_STEPS = 4
DEPTH = 2
FULL = 63
QUERY_LIMIT = 62
HALO = 32
LOG2E = math.log2(math.e)
NEG = -1e30
MIB = 1 << 20
BF = jnp.bfloat16
F32 = jnp.float32


def vmem():
    return pl.BlockSpec(memory_space=pltpu.VMEM)


def anywhere():
    return pl.BlockSpec(memory_space=pl.ANY)


def params(limit=48):
    return pltpu.CompilerParams(vmem_limit_bytes=limit * MIB)


def iota(shape, dim):
    return lax.broadcasted_iota(jnp.int32, shape, dim)


def pool_kernel(len_hbm, gain_hbm, enc_hbm, wk_hbm, wv_hbm, kv_ref, x_hbm, scale_ref, lengths, gain, enc, wkv, x, sems):
    byte_rows, width = enc.shape
    block = width // POOL_STEPS
    small = [
        pltpu.make_async_copy(len_hbm, lengths, sems.at[0]),
        pltpu.make_async_copy(gain_hbm, gain, sems.at[1]),
    ]
    for copy in small:
        copy.start()
    copies = []
    for step in range(POOL_STEPS):
        part = pl.ds(step * block, block)
        at = 2 + 3 * step
        group = [
            pltpu.make_async_copy(enc_hbm.at[:, part], enc.at[:, part], sems.at[at]),
            pltpu.make_async_copy(wk_hbm.at[part], wkv.at[part, pl.ds(0, HD)], sems.at[at + 1]),
            pltpu.make_async_copy(wv_hbm.at[part], wkv.at[part, pl.ds(HD, HD)], sems.at[at + 2]),
        ]
        copies.append(group)
        if step < DEPTH:
            for copy in group:
                copy.start()
    for copy in small:
        copy.wait()
    before = iota((CAP, CAP), 1) < iota((CAP, CAP), 0)
    start = jnp.sum(jnp.where(before, lengths[...], 0).astype(F32), axis=1, keepdims=True)
    hot = jnp.where(iota((CAP, byte_rows), 1).astype(F32) == start, 1.0, 0.0).astype(BF)
    total = jnp.zeros((CAP, 2 * HD), F32)
    squares = jnp.zeros((CAP, HD), F32)
    leaving = []
    held = None
    for step in range(POOL_STEPS + 1):
        if step < POOL_STEPS:
            for copy in copies[step]:
                copy.wait()
            if step + DEPTH < POOL_STEPS:
                for copy in copies[step + DEPTH]:
                    copy.start()
        if held is not None:
            last = slice((step - 1) * block, step * block)
            total += jnp.dot(held, wkv[last, :], preferred_element_type=F32)
        if step < POOL_STEPS:
            part = slice(step * block, (step + 1) * block)
            pooled = jnp.dot(hot, enc[:, part], preferred_element_type=F32)
            for k in range(block // HD):
                piece = pooled[:, k * HD : (k + 1) * HD]
                squares += piece * piece
            held = (pooled * gain[:, part]).astype(BF)
            x[:, part] = held
            leaving.append(
                pltpu.make_async_copy(
                    x.at[:, pl.ds(step * block, block)],
                    x_hbm.at[:, pl.ds(step * block, block)],
                    sems.at[2 + 3 * POOL_STEPS + step],
                )
            )
            leaving[-1].start()
    scale = lax.rsqrt(jnp.sum(squares, axis=1, keepdims=True) / width + 1e-5)
    scale_ref[...] = jnp.broadcast_to(scale, scale_ref.shape)
    kv_ref[:CAP, :] = (total * scale).astype(BF)
    count = jnp.sum((lengths[...] > 0).astype(F32), axis=1, keepdims=True)
    kv_ref[CAP:, :] = jnp.broadcast_to(count, (TILE, 2 * HD)).astype(BF)
    for copy in leaving:
        copy.wait()


def pool(lengths, enc, gain, wk, wv):
    byte_rows, width = enc.shape
    return pl.pallas_call(
        pool_kernel,
        in_specs=[anywhere()] * 5,
        out_specs=[vmem(), anywhere(), vmem()],
        out_shape=[
            jax.ShapeDtypeStruct((ROWS, 2 * HD), BF),
            jax.ShapeDtypeStruct((CAP, width), BF),
            jax.ShapeDtypeStruct((CAP, HD), F32),
        ],
        scratch_shapes=[
            pltpu.VMEM(lengths.shape, jnp.int32),
            pltpu.VMEM(gain.shape, F32),
            pltpu.VMEM((byte_rows, width), BF),
            pltpu.VMEM((width, 2 * HD), BF),
            pltpu.VMEM((CAP, width), BF),
            pltpu.SemaphoreType.DMA((4 * POOL_STEPS + 2,)),
        ],
        compiler_params=params(FULL),
        cost_estimate=pl.CostEstimate(
            flops=2 * CAP * width * (byte_rows + 2 * HD),
            bytes_accessed=2 * width * (byte_rows + CAP + 2 * HD),
            transcendentals=0,
        ),
        name="pool",
    )(lengths, gain, enc, wk, wv)


def query_kernel(x_hbm, scale_ref, wq_hbm, q_ref, x, wq, sems):
    width = wq.shape[0]
    block = width // POOL_STEPS
    copies = []
    for step in range(POOL_STEPS):
        part = pl.ds(step * block, block)
        copies.append(
            [
                pltpu.make_async_copy(wq_hbm.at[part], wq.at[part], sems.at[2 * step]),
                pltpu.make_async_copy(x_hbm.at[:, part], x.at[:, part], sems.at[2 * step + 1]),
            ]
        )
        for copy in copies[-1]:
            copy.start()
    total = jnp.zeros(q_ref.shape, F32)
    for step in range(POOL_STEPS):
        for copy in copies[step]:
            copy.wait()
        part = slice(step * block, (step + 1) * block)
        total += jnp.dot(x[:, part], wq[part, :], preferred_element_type=F32)
    q_ref[...] = (total * (scale_ref[:, :1] * (LOG2E * HD**-0.5))).astype(BF)


def query(x, wq, scale):
    width, out = wq.shape
    return pl.pallas_call(
        query_kernel,
        in_specs=[anywhere(), vmem(), anywhere()],
        out_specs=vmem(),
        out_shape=jax.ShapeDtypeStruct((CAP, out), BF),
        scratch_shapes=[
            pltpu.VMEM((CAP, width), BF),
            pltpu.VMEM((width, out), BF),
            pltpu.SemaphoreType.DMA((2 * POOL_STEPS,)),
        ],
        compiler_params=params(QUERY_LIMIT),
        cost_estimate=pl.CostEstimate(
            flops=2 * CAP * width * out, bytes_accessed=2 * width * (out + CAP), transcendentals=0
        ),
        name="query",
    )(x, scale, wq)


def compact_kernel(index_ref, *refs):
    blocks, out_ref = refs[:8], refs[8]
    x, core = index_ref[1], index_ref[2]
    shifts = (0, 1, 3, 2)
    order = [
        ((x + NX - shift) % NX) * 2 + (core if side == 0 else 1 - core)
        for side in range(2)
        for shift in shifts
    ]
    counts = [ref[CAP : CAP + TILE, :].astype(F32)[:1, :] for ref in blocks]
    lane = iota((1, CAP), 1).astype(F32)
    targets = []
    for i in range(8):
        first = jnp.zeros((1, 2 * HD), F32)
        for k in range(8):
            if k != i:
                first += jnp.where(order[k] < order[i], counts[k], 0.0)
        targets.append(jnp.where(lane < counts[i][:, :CAP], first[:, :CAP] + lane, -1.0))
    sub = iota((TILE, 2 * HD), 0)
    table = jnp.zeros((TILE, 2 * HD), F32)
    for i in range(8):
        table += jnp.where(sub == order[i], counts[i], 0.0)
    out_ref[HALF:UPPER, :] = table.astype(BF)
    for half in range(2):
        row = (iota((HALF, CAP), 0) + half * HALF).astype(F32)
        total = jnp.zeros((HALF, 2 * HD), F32)
        for i in range(8):
            hot = jnp.where(row == targets[i], 1.0, 0.0).astype(BF)
            total += jnp.dot(hot, blocks[i][:CAP, :], preferred_element_type=F32)
        out_ref[half * UPPER : half * UPPER + HALF, :] = total.astype(BF)


def compact(index, blocks):
    return pl.pallas_call(
        compact_kernel,
        in_specs=[pl.BlockSpec(memory_space=pltpu.SMEM)] + [vmem()] * 8,
        out_specs=vmem(),
        out_shape=jax.ShapeDtypeStruct((PIECE, 2 * HD), BF),
        compiler_params=params(),
        name="compact",
    )(index, *blocks)


def single(value):
    return jnp.max(jnp.sum(value, axis=0, keepdims=True)).astype(jnp.int32)


def table_of(ref):
    return ref[HALF:UPPER, :HD].astype(F32)


def heads_of(q_ref, slots):
    q = jnp.concatenate([q_ref[slots, h * HD : (h + 1) * HD] for h in range(4)], axis=0)
    ones = jnp.where(iota((4 * QT, HD), 1) == 0, 1.0, 0.0).astype(BF)
    return jnp.concatenate([q, ones], axis=1)


def place(keys, values, ref, low, to_row, first, live):
    to = pl.ds(pl.multiple_of(first + to_row, TILE), HALF)
    keys[to, :HD] = ref[low : low + HALF, :HD]
    values[to, :] = ref[low : low + HALF, HD:]
    dead = jnp.where(iota((HALF, HD), 0) + to_row < live, 0.0, NEG)
    keys[to, HD:] = dead.astype(BF)


def fill(keys, values, start, rows, bias):
    end = pl.ds(pl.multiple_of(start, TILE), rows)
    keys[end, :HD] = jnp.zeros((rows, HD), BF)
    keys[end, HD:] = jnp.full((rows, HD), bias, BF)
    values[end, :] = jnp.zeros((rows, HD), BF)


def softmax_chunks(q, query_pos, free, chunks, keys, values, scores, top, lsum, acc):
    def score(c):
        rows = pl.ds(pl.multiple_of(c * KEYS, KEYS), KEYS)
        return lax.dot_general(
            q, keys[rows, :], (((1,), (1,)), ((), ())), preferred_element_type=F32
        )

    def keep(c, s):
        scores[c] = s
        best = top[...]
        for k in range(KEYS // HD):
            best = jnp.maximum(best, s[:, k * HD : (k + 1) * HD])
        top[...] = best

    def open_chunk(c, _):
        keep(c, score(c))
        return 0

    def masked_chunk(c, _):
        allowed = c * KEYS + iota((4 * QT, KEYS), 1) <= query_pos
        keep(c, jnp.where(allowed, score(c), NEG))
        return 0

    lax.fori_loop(0, free, open_chunk, 0)
    if query_pos is not None:
        lax.fori_loop(free, chunks, masked_chunk, 0)
    top[...] = jnp.broadcast_to(jnp.max(top[...], axis=1, keepdims=True), top.shape)

    def weigh(c, _):
        best = top[...]
        parts = [jnp.exp2(scores[c, :, k * HD : (k + 1) * HD] - best) for k in range(KEYS // HD)]
        total = parts[0]
        for part in parts[1:]:
            total = total + part
        lsum[...] += total
        p = jnp.concatenate([part.astype(BF) for part in parts], axis=1)
        rows = pl.ds(pl.multiple_of(c * KEYS, KEYS), KEYS)
        acc[...] += jnp.dot(p, values[rows, :], preferred_element_type=F32)
        return 0

    return weigh


def attend_near_kernel(index_ref, q_ref, *refs):
    pieces, (top, lsum, acc, info_ref) = refs[:7], refs[7:11]
    keys, values, scores = refs[11:]
    z, x, core = index_ref[0], index_ref[1], index_ref[2]
    own = x * 2 + core

    own_piece, came, swapped = pieces[0], pieces[1:4], pieces[4:7]
    upward, downward = (came, swapped), (swapped, came)
    planes = [(8 - s, [downward[c][s - 1] for c in range(2)]) for s in (1, 2, 3)]
    planes += [(s, [upward[c][s - 1] for c in range(2)]) for s in (3, 2, 1)]
    planes.append((0, [own_piece, own_piece]))

    lives, most = [], jnp.int32(0)
    for back, (a, b) in planes:
        table = jnp.where(core == 0, table_of(a), table_of(b)) if back else table_of(a)
        lives.append(single(table))
        most = jnp.maximum(most, lives[-1])
    row = iota((TILE, HD), 0)
    own_table = table_of(own_piece)
    before = single(jnp.where(row < own, own_table, 0.0))
    count = single(jnp.where(row == own, own_table, 0.0))
    info_ref[0] = most
    info_ref[1] = count

    first = jnp.int32(0)
    for (back, where), live in zip(planes, lives):
        here = jnp.minimum(live, 2 * HALF)
        for c in range(2 if back else 1):
            wanted = (z >= back) & (core == c) if back else z >= 0

            @pl.when(wanted)
            def _(ref=where[c], here=here, first=first):
                place(keys, values, ref, 0, 0, first, here)
                place(keys, values, ref, UPPER, HALF, first, here)

        if back:
            first = first + jnp.where(z >= back, (here + TILE - 1) // TILE * TILE, 0)
    fill(keys, values, first + 2 * HALF, KEYS, 0.0)
    free = first // KEYS
    chunks = (first + jnp.minimum(before + count, 2 * HALF) + KEYS - 1) // KEYS

    def per_tile(tile, _):
        slots = pl.ds(pl.multiple_of(tile * QT, QT), QT)
        mine = [ref.at[tile] for ref in (top, lsum, acc)]
        mine[0][...] = jnp.full((4 * QT, HD), NEG, F32)
        mine[1][...] = jnp.zeros((4 * QT, HD), F32)
        mine[2][...] = jnp.zeros((4 * QT, HD), F32)
        query_pos = first + before + tile * QT + iota((4 * QT, 1), 0) % QT
        weigh = softmax_chunks(
            heads_of(q_ref, slots), query_pos, free, chunks, keys, values, scores, *mine
        )
        lax.fori_loop(0, chunks, weigh, 0)
        return 0

    lax.fori_loop(0, (count + QT - 1) // QT, per_tile, 0)


def attend_near(index, q, pieces):
    most = 7 * 2 * HALF + KEYS
    most = (most + KEYS - 1) // KEYS * KEYS
    return pl.pallas_call(
        attend_near_kernel,
        in_specs=[pl.BlockSpec(memory_space=pltpu.SMEM)] + [vmem()] * (1 + len(pieces)),
        out_specs=[vmem()] * 3 + [pl.BlockSpec(memory_space=pltpu.SMEM)],
        out_shape=[jax.ShapeDtypeStruct((CAP // QT, 4 * QT, HD), F32)] * 3
        + [jax.ShapeDtypeStruct((2,), jnp.int32)],
        scratch_shapes=[
            pltpu.VMEM((most, 2 * HD), BF),
            pltpu.VMEM((most, HD), BF),
            pltpu.VMEM((most // KEYS, 4 * QT, KEYS), F32),
        ],
        compiler_params=params(),
        cost_estimate=pl.CostEstimate(
            flops=12 * QT * most * 3 * HD * 2, bytes_accessed=1 << 23, transcendentals=8 * QT * most
        ),
        name="attend_near",
    )(index, q, *pieces)


def attend_far_kernel(index_ref, info_ref, q_ref, wout_ref, came, swapped, top, lsum, acc, *refs):
    outs, flag_ref = refs[:4], refs[4]
    keys, values, scores, peak, total, sums = refs[5:]
    z, core, y = index_ref[0], index_ref[2], index_ref[3]
    for out in outs:
        out[...] = jnp.zeros_like(out)
    live = single(table_of_far(came, core))
    flag_ref[0] = (jnp.maximum(info_ref[0], live) > 2 * HALF).astype(jnp.int32)
    count = info_ref[1]
    here = jnp.minimum(live, 2 * HALF)
    for c, lower, upper in ((0, came, swapped), (1, swapped, came)):

        @pl.when(core == c)
        def _(lower=lower, upper=upper):
            place(keys, values, lower, 0, 0, 0, here)
            place(keys, values, upper, TILE, HALF, 0, here)

    fill(keys, values, 2 * HALF, 2 * KEYS - 2 * HALF, NEG)
    chunks = jnp.where(z >= 4, (here + KEYS - 1) // KEYS, 0)

    def per_tile(tile, _):
        slots = pl.ds(pl.multiple_of(tile * QT, QT), QT)
        peak[...] = top[tile]
        weigh = softmax_chunks(
            heads_of(q_ref, slots), None, chunks, chunks, keys, values, scores, peak, total, sums
        )
        factor = jnp.exp2(top[tile] - peak[...])
        total[...] = lsum[tile] * factor
        sums[...] = acc[tile] * factor
        lax.fori_loop(0, chunks, weigh, 0)
        a = (sums[...] / jnp.sum(total[...], axis=1, keepdims=True)).astype(BF)
        a = jnp.concatenate([a[h * QT : (h + 1) * QT, :] for h in range(4)], axis=1)
        for k in range(4):
            cols = pl.ds(pl.multiple_of(((y + k) % 4) * 256, 256), 256)
            outs[k][slots, :] = jnp.dot(
                a, wout_ref[:, cols], preferred_element_type=F32
            ).astype(BF)
        return 0

    lax.fori_loop(0, (count + QT - 1) // QT, per_tile, 0)


def table_of_far(came, core):
    low, high = came[:TILE, :HD].astype(F32), came[HALF:UPPER, :HD].astype(F32)
    return jnp.where(core == 0, high, low)


def attend_far(index, info, q, wout, came, swapped, state):
    *parts, flag = pl.pallas_call(
        attend_far_kernel,
        in_specs=[pl.BlockSpec(memory_space=pltpu.SMEM)] * 2 + [vmem()] * 7,
        out_specs=[vmem()] * 4 + [pl.BlockSpec(memory_space=pltpu.SMEM)],
        out_shape=[jax.ShapeDtypeStruct((CAP, 256), BF)] * 4
        + [jax.ShapeDtypeStruct((1,), jnp.int32)],
        scratch_shapes=[
            pltpu.VMEM((2 * KEYS, 2 * HD), BF),
            pltpu.VMEM((2 * KEYS, HD), BF),
            pltpu.VMEM((2, 4 * QT, KEYS), F32),
        ]
        + [pltpu.VMEM((4 * QT, HD), F32)] * 3,
        compiler_params=params(),
        name="attend_far",
    )(index, info, q, wout, came, swapped, *state)
    return parts, flag[0]


def attend_any(kv, q, lengths, wout, y):
    device = lax.axis_index("seq")
    devices = lax.axis_size("seq")
    queries = q.reshape(CAP, 4, HD)
    slot = jnp.arange(CAP, dtype=jnp.int32)

    def step(turn, carry):
        block, top, total, weighted = carry
        source = (device - turn) % devices
        keys, values = block[:CAP, :HD], block[:CAP, HD:]
        live = block[CAP, 0].astype(jnp.int32)
        s = jnp.einsum("wgd,rd->wgr", queries, keys, preferred_element_type=F32)
        later = (source == device) & (slot[None, :] > slot[:, None])
        allowed = ((slot < live)[None, :] & (source <= device) & ~later)[:, None, :]
        s = jnp.where(allowed, s, NEG)
        new = jnp.maximum(top, jnp.max(s, axis=2))
        factor = jnp.exp2(top - new)
        w = jnp.where(allowed, jnp.exp2(s - new[..., None]), 0.0)
        total = total * factor + jnp.sum(w, axis=2)
        weighted = weighted * factor[..., None] + jnp.einsum(
            "wgr,rd->wgd", w.astype(BF), values, preferred_element_type=F32
        )
        block = lax.ppermute(block, "seq", [(i, (i + 1) % devices) for i in range(devices)])
        return block, new, total, weighted

    start = (
        kv,
        jnp.full((CAP, 4), NEG, F32),
        jnp.zeros((CAP, 4), F32),
        jnp.zeros((CAP, 4, HD), F32),
    )
    _, _, total, weighted = lax.fori_loop(0, devices, step, start)
    a = (weighted / total[..., None]).reshape(CAP, 4 * HD).astype(BF)
    part = jnp.dot(a, wout, preferred_element_type=F32).astype(BF)
    return [lax.dynamic_slice_in_dim(part, ((y + k) % 4) * 256, 256, 1) for k in range(4)]


def mix_kernel(len_ref, skip_ref, p0, p1, p2, p3, mixed_ref, tail_ref):
    byte_rows = skip_ref.shape[0]
    lengths = len_ref[...].astype(F32)
    inner = p0[...].astype(F32) + p1[...].astype(F32) + p2[...].astype(F32) + p3[...].astype(F32)
    i, j = iota((CAP, CAP), 0), iota((CAP, CAP), 1)
    column = jnp.sum(jnp.where(i == j, lengths, 0.0), axis=1, keepdims=True)
    start = jnp.sum(jnp.where(i < j, column, 0.0), axis=0, keepdims=True)
    at = iota((byte_rows, CAP), 0).astype(F32)
    hot = jnp.where((at >= start) & (at < start + lengths), 1.0, 0.0).astype(BF)
    up = jnp.dot(hot, inner.astype(BF), preferred_element_type=F32)
    mixed = (skip_ref[...].astype(F32) + up).astype(BF)
    mixed_ref[...] = mixed
    tail_ref[...] = mixed[byte_rows - HALO :, :]


def mix(lengths, skip, parts):
    return pl.pallas_call(
        mix_kernel,
        in_specs=[vmem()] * 6,
        out_specs=[vmem()] * 2,
        out_shape=[
            jax.ShapeDtypeStruct(skip.shape, BF),
            jax.ShapeDtypeStruct((HALO, skip.shape[1]), BF),
        ],
        compiler_params=params(),
        name="mix",
    )(lengths, skip, *parts)


def filtered(window, taps):
    rows = window.shape[0] - HALO
    total = jnp.zeros((rows, window.shape[1]), F32)
    lags = taps.shape[0]
    for r in range(8):
        moved = window[8 - r : rows + HALO - r, :]
        for lag in range(r, lags, 8):
            low = HALO - 8 - (lag - r)
            total += taps[lag : lag + 1, :] * moved[low : low + rows, :]
    return (window[HALO:, :] + total / (1.0 + jnp.exp(-total))).astype(BF)


def conv_kernel(mixed_ref, taps_ref, out_ref, ext):
    byte_rows, channels = mixed_ref.shape
    ext[:HALO, :] = jnp.zeros((HALO, channels), F32)
    ext[HALO:, :] = mixed_ref[...].astype(F32)
    block = 64

    def per_block(i, _):
        first = pl.multiple_of(i * block, block)
        for low in range(0, channels, 128):
            part = slice(low, low + 128)
            window = ext[pl.ds(first, block + HALO), part]
            out_ref[pl.ds(first, block), part] = filtered(window, taps_ref[:, part])
        return 0

    lax.fori_loop(0, byte_rows // block, per_block, 0)


def rim_kernel(given_hbm, rim_ref, mixed_ref, taps_ref, out_hbm, rows, sem):
    del given_hbm
    for low in range(0, mixed_ref.shape[1], 128):
        part = slice(low, low + 128)
        window = jnp.concatenate([rim_ref[:, part], mixed_ref[:HALO, part]], axis=0).astype(F32)
        rows[:, part] = filtered(window, taps_ref[:, part])
    copy = pltpu.make_async_copy(rows, out_hbm.at[pl.ds(0, HALO)], sem)
    copy.start()
    copy.wait()


def convolve(mixed, taps):
    return pl.pallas_call(
        conv_kernel,
        in_specs=[vmem()] * 2,
        out_specs=vmem(),
        out_shape=jax.ShapeDtypeStruct(mixed.shape, BF),
        scratch_shapes=[pltpu.VMEM((HALO + mixed.shape[0], mixed.shape[1]), F32)],
        compiler_params=params(),
        cost_estimate=pl.CostEstimate(
            flops=2 * mixed.size * taps.shape[0], bytes_accessed=16 * mixed.size, transcendentals=0
        ),
        name="convolve",
    )(mixed, taps)


def first_rows(given, rim, mixed, taps):
    return pl.pallas_call(
        rim_kernel,
        in_specs=[anywhere()] + [vmem()] * 3,
        out_specs=anywhere(),
        out_shape=jax.ShapeDtypeStruct(given.shape, BF),
        input_output_aliases={0: 0},
        scratch_shapes=[pltpu.VMEM((HALO, mixed.shape[1]), BF), pltpu.SemaphoreType.DMA],
        compiler_params=params(),
        name="first_rows",
    )(given, rim, mixed, taps)


def seq_permute(value, move):
    pairs = []
    for z in range(NZ):
        for x in range(NX):
            for core in range(2):
                tz, tx, tc = move(z, x, core)
                target = ((tz % NZ) * NX + tx % NX) * 2 + tc
                pairs.append(((z * NX + x) * 2 + core, target))
    return lax.ppermute(value, "seq", pairs)


def along_x(value, steps):
    return seq_permute(value, lambda z, x, c: (z, x + steps, c))


def round_z(value):
    return seq_permute(value, lambda z, x, c: (z + 1 - 2 * c, x, c))


def swap(value):
    return seq_permute(value, lambda z, x, c: (z, x, 1 - c))


def per_device(enc, span_len, skip, gain, wq, wk, wv, wout, taps):
    seq = lax.axis_index("seq")
    y = lax.axis_index("section")
    index = jnp.stack([seq // (2 * NX), (seq // 2) % NX, seq % 2, y]).astype(jnp.int32)
    kv, x, scale = pool(span_len, enc, gain.reshape(1, -1), wk, wv)
    column = [kv, along_x(kv, 1), along_x(kv, -1), along_x(kv, 2)]
    plane = compact(index, column + [swap(v) for v in column])
    first, q = lax.optimization_barrier((round_z(plane), query(x, wq, scale)))
    came = [first]
    came.append(round_z(came[-1]))
    came.append(round_z(came[-1]))
    far = round_z(lax.dynamic_slice_in_dim(came[-1], (seq % 2) * HALF, UPPER, 0))
    near = attend_near(index, q, [plane] + came + [swap(piece) for piece in came])
    far, (*state, info) = lax.optimization_barrier((far, near))
    parts, crowded = attend_far(index, info, q, wout, far, swap(far), state)
    parts = lax.cond(
        crowded > 0, lambda _: attend_any(kv, q, span_len, wout, y), lambda given: given, parts
    )
    sent = [
        lax.ppermute(parts[k], "section", [(i, (i + k) % 4) for i in range(4)]) for k in (1, 2, 3)
    ]
    mixed, tail = mix(span_len, skip, [parts[0]] + sent)
    rim = lax.ppermute(tail, "seq", [(i, i + 1) for i in range(2 * NX * NZ - 1)])
    return first_rows(convolve(mixed, taps), rim, mixed, taps)


def solution(mesh):
    return jax.shard_map(
        per_device,
        mesh=mesh,
        in_specs=(
            P("seq", None),
            P("seq", None),
            P("seq", "section"),
            P(),
            P(None, "section"),
            P(None, "section"),
            P(None, "section"),
            P("section", None),
            P(None, "section"),
        ),
        out_specs=P("seq", "section"),
        check_vma=False,
    )
```

```python
import math

import jax
import jax.numpy as jnp
from jax import lax
from jax.experimental import pallas as pl
from jax.experimental.pallas import tpu as pltpu
from jax.sharding import PartitionSpec as P

HD = 128
CAP = 192
TILE = 16
ROWS = CAP + TILE
NX = 4
NZ = 8
HALF = 352
UPPER = HALF + TILE
PIECE = UPPER + HALF
QT = 96
KEYS = 512
POOL_STEPS = 4
DEPTH = 4
FULL = 62
QUERY_LIMIT = 60
HALO = 32
LOG2E = math.log2(math.e)
NEG = -1e30
MIB = 1 << 20
BF = jnp.bfloat16
F32 = jnp.float32


def vmem():
    return pl.BlockSpec(memory_space=pltpu.VMEM)


def anywhere():
    return pl.BlockSpec(memory_space=pl.ANY)


def params(limit=48):
    return pltpu.CompilerParams(vmem_limit_bytes=limit * MIB)


def iota(shape, dim):
    return lax.broadcasted_iota(jnp.int32, shape, dim)


def pool_kernel(len_hbm, gain_hbm, enc_hbm, wk_hbm, wv_hbm, kv_ref, x_ref, scale_ref, lengths, gain, enc, wkv, sems):
    byte_rows, width = enc.shape
    block = width // POOL_STEPS
    small = [
        pltpu.make_async_copy(len_hbm, lengths, sems.at[0]),
        pltpu.make_async_copy(gain_hbm, gain, sems.at[1]),
    ]
    for copy in small:
        copy.start()
    copies = []
    for step in range(POOL_STEPS):
        part = pl.ds(step * block, block)
        at = 2 + 3 * step
        group = [
            pltpu.make_async_copy(enc_hbm.at[:, part], enc.at[:, part], sems.at[at]),
            pltpu.make_async_copy(wk_hbm.at[part], wkv.at[part, pl.ds(0, HD)], sems.at[at + 1]),
            pltpu.make_async_copy(wv_hbm.at[part], wkv.at[part, pl.ds(HD, HD)], sems.at[at + 2]),
        ]
        copies.append(group)
        if step < DEPTH:
            for copy in group:
                copy.start()
    for copy in small:
        copy.wait()
    before = iota((CAP, CAP), 1) < iota((CAP, CAP), 0)
    start = jnp.sum(jnp.where(before, lengths[...], 0).astype(F32), axis=1, keepdims=True)
    hot = jnp.where(iota((CAP, byte_rows), 1).astype(F32) == start, 1.0, 0.0).astype(BF)
    total = jnp.zeros((CAP, 2 * HD), F32)
    squares = jnp.zeros((CAP, HD), F32)
    held = None
    for step in range(POOL_STEPS + 1):
        if step < POOL_STEPS:
            for copy in copies[step]:
                copy.wait()
            if step + DEPTH < POOL_STEPS:
                for copy in copies[step + DEPTH]:
                    copy.start()
        if held is not None:
            last = slice((step - 1) * block, step * block)
            total += jnp.dot(held, wkv[last, :], preferred_element_type=F32)
        if step < POOL_STEPS:
            part = slice(step * block, (step + 1) * block)
            pooled = jnp.dot(hot, enc[:, part], preferred_element_type=F32)
            for k in range(block // HD):
                piece = pooled[:, k * HD : (k + 1) * HD]
                squares += piece * piece
            held = (pooled * gain[:, part]).astype(BF)
            x_ref[:, part] = held
    scale = lax.rsqrt(jnp.sum(squares, axis=1, keepdims=True) / width + 1e-5)
    scale_ref[...] = jnp.broadcast_to(scale, scale_ref.shape)
    kv_ref[:CAP, :] = (total * scale).astype(BF)
    count = jnp.sum((lengths[...] > 0).astype(F32), axis=1, keepdims=True)
    kv_ref[CAP:, :] = jnp.broadcast_to(count, (TILE, 2 * HD)).astype(BF)


def pool(lengths, enc, gain, wk, wv):
    byte_rows, width = enc.shape
    return pl.pallas_call(
        pool_kernel,
        in_specs=[anywhere()] * 5,
        out_specs=[vmem()] * 3,
        out_shape=[
            jax.ShapeDtypeStruct((ROWS, 2 * HD), BF),
            jax.ShapeDtypeStruct((CAP, width), BF),
            jax.ShapeDtypeStruct((CAP, HD), F32),
        ],
        scratch_shapes=[
            pltpu.VMEM(lengths.shape, jnp.int32),
            pltpu.VMEM(gain.shape, F32),
            pltpu.VMEM((byte_rows, width), BF),
            pltpu.VMEM((width, 2 * HD), BF),
            pltpu.SemaphoreType.DMA((3 * POOL_STEPS + 2,)),
        ],
        compiler_params=params(FULL),
        cost_estimate=pl.CostEstimate(
            flops=2 * CAP * width * (byte_rows + 2 * HD),
            bytes_accessed=2 * width * (byte_rows + CAP + 2 * HD),
            transcendentals=0,
        ),
        name="pool",
    )(lengths, gain, enc, wk, wv)


def query_kernel(x_ref, scale_ref, wq_hbm, q_ref, wq, sems):
    width = wq.shape[0]
    block = width // POOL_STEPS
    copies = []
    for step in range(POOL_STEPS):
        part = pl.ds(step * block, block)
        copies.append(pltpu.make_async_copy(wq_hbm.at[part], wq.at[part], sems.at[step]))
        copies[-1].start()
    total = jnp.zeros(q_ref.shape, F32)
    for step in range(POOL_STEPS):
        copies[step].wait()
        part = slice(step * block, (step + 1) * block)
        total += jnp.dot(x_ref[:, part], wq[part, :], preferred_element_type=F32)
    q_ref[...] = (total * (scale_ref[:, :1] * (LOG2E * HD**-0.5))).astype(BF)


def query(x, wq, scale):
    width, out = wq.shape
    return pl.pallas_call(
        query_kernel,
        in_specs=[vmem(), vmem(), anywhere()],
        out_specs=vmem(),
        out_shape=jax.ShapeDtypeStruct((CAP, out), BF),
        scratch_shapes=[
            pltpu.VMEM((width, out), BF),
            pltpu.SemaphoreType.DMA((POOL_STEPS,)),
        ],
        compiler_params=params(QUERY_LIMIT),
        cost_estimate=pl.CostEstimate(
            flops=2 * CAP * width * out, bytes_accessed=2 * width * (out + CAP), transcendentals=0
        ),
        name="query",
    )(x, scale, wq)


def compact_kernel(index_ref, *refs):
    blocks, out_ref = refs[:8], refs[8]
    x, core = index_ref[1], index_ref[2]
    shifts = (0, 1, 3, 2)
    order = [
        ((x + NX - shift) % NX) * 2 + (core if side == 0 else 1 - core)
        for side in range(2)
        for shift in shifts
    ]
    counts = [ref[CAP : CAP + TILE, :].astype(F32)[:1, :] for ref in blocks]
    lane = iota((1, CAP), 1).astype(F32)
    targets = []
    for i in range(8):
        first = jnp.zeros((1, 2 * HD), F32)
        for k in range(8):
            if k != i:
                first += jnp.where(order[k] < order[i], counts[k], 0.0)
        targets.append(jnp.where(lane < counts[i][:, :CAP], first[:, :CAP] + lane, -1.0))
    sub = iota((TILE, 2 * HD), 0)
    table = jnp.zeros((TILE, 2 * HD), F32)
    for i in range(8):
        table += jnp.where(sub == order[i], counts[i], 0.0)
    out_ref[HALF:UPPER, :] = table.astype(BF)
    for half in range(2):
        row = (iota((HALF, CAP), 0) + half * HALF).astype(F32)
        total = jnp.zeros((HALF, 2 * HD), F32)
        for i in range(8):
            hot = jnp.where(row == targets[i], 1.0, 0.0).astype(BF)
            total += jnp.dot(hot, blocks[i][:CAP, :], preferred_element_type=F32)
        out_ref[half * UPPER : half * UPPER + HALF, :] = total.astype(BF)


def compact(index, blocks):
    return pl.pallas_call(
        compact_kernel,
        in_specs=[pl.BlockSpec(memory_space=pltpu.SMEM)] + [vmem()] * 8,
        out_specs=vmem(),
        out_shape=jax.ShapeDtypeStruct((PIECE, 2 * HD), BF),
        compiler_params=params(),
        name="compact",
    )(index, *blocks)


def single(value):
    return jnp.max(jnp.sum(value, axis=0, keepdims=True)).astype(jnp.int32)


def table_of(ref):
    return ref[HALF:UPPER, :HD].astype(F32)


def heads_of(q_ref, slots):
    q = jnp.concatenate([q_ref[slots, h * HD : (h + 1) * HD] for h in range(4)], axis=0)
    ones = jnp.where(iota((4 * QT, HD), 1) == 0, 1.0, 0.0).astype(BF)
    return jnp.concatenate([q, ones], axis=1)


def place(keys, values, ref, low, to_row, first, live):
    to = pl.ds(pl.multiple_of(first + to_row, TILE), HALF)
    keys[to, :HD] = ref[low : low + HALF, :HD]
    values[to, :] = ref[low : low + HALF, HD:]
    dead = jnp.where(iota((HALF, HD), 0) + to_row < live, 0.0, NEG)
    keys[to, HD:] = dead.astype(BF)


def fill(keys, values, start, rows, bias):
    end = pl.ds(pl.multiple_of(start, TILE), rows)
    keys[end, :HD] = jnp.zeros((rows, HD), BF)
    keys[end, HD:] = jnp.full((rows, HD), bias, BF)
    values[end, :] = jnp.zeros((rows, HD), BF)


def softmax_chunks(q, query_pos, free, chunks, keys, values, scores, top, lsum, acc):
    def score(c):
        rows = pl.ds(pl.multiple_of(c * KEYS, KEYS), KEYS)
        return lax.dot_general(
            q, keys[rows, :], (((1,), (1,)), ((), ())), preferred_element_type=F32
        )

    def keep(c, s):
        scores[c] = s
        best = top[...]
        for k in range(KEYS // HD):
            best = jnp.maximum(best, s[:, k * HD : (k + 1) * HD])
        top[...] = best

    def open_chunk(c, _):
        keep(c, score(c))
        return 0

    def masked_chunk(c, _):
        allowed = c * KEYS + iota((4 * QT, KEYS), 1) <= query_pos
        keep(c, jnp.where(allowed, score(c), NEG))
        return 0

    lax.fori_loop(0, free, open_chunk, 0)
    if query_pos is not None:
        lax.fori_loop(free, chunks, masked_chunk, 0)
    top[...] = jnp.broadcast_to(jnp.max(top[...], axis=1, keepdims=True), top.shape)

    def weigh(c, _):
        best = top[...]
        parts = [jnp.exp2(scores[c, :, k * HD : (k + 1) * HD] - best) for k in range(KEYS // HD)]
        total = parts[0]
        for part in parts[1:]:
            total = total + part
        lsum[...] += total
        p = jnp.concatenate([part.astype(BF) for part in parts], axis=1)
        rows = pl.ds(pl.multiple_of(c * KEYS, KEYS), KEYS)
        acc[...] += jnp.dot(p, values[rows, :], preferred_element_type=F32)
        return 0

    return weigh


def attend_near_kernel(index_ref, q_ref, *refs):
    pieces, (top, lsum, acc, info_ref) = refs[:5], refs[5:9]
    keys, values, scores = refs[9:]
    z, x, core = index_ref[0], index_ref[1], index_ref[2]
    own = x * 2 + core

    own_piece, came, swapped = pieces[0], pieces[1:3], pieces[3:5]
    upward, downward = (came, swapped), (swapped, came)
    planes = [(8 - s, [downward[c][s - 1] for c in range(2)]) for s in (1, 2)]
    planes += [(s, [upward[c][s - 1] for c in range(2)]) for s in (2, 1)]
    planes.append((0, [own_piece, own_piece]))

    lives, most = [], jnp.int32(0)
    for back, (a, b) in planes:
        table = jnp.where(core == 0, table_of(a), table_of(b)) if back else table_of(a)
        lives.append(single(table))
        most = jnp.maximum(most, lives[-1])
    row = iota((TILE, HD), 0)
    own_table = table_of(own_piece)
    before = single(jnp.where(row < own, own_table, 0.0))
    count = single(jnp.where(row == own, own_table, 0.0))
    info_ref[0] = most
    info_ref[1] = count

    first = jnp.int32(0)
    for (back, where), live in zip(planes, lives):
        here = jnp.minimum(live, 2 * HALF)
        for c in range(2 if back else 1):
            wanted = (z >= back) & (core == c) if back else z >= 0

            @pl.when(wanted)
            def _(ref=where[c], here=here, first=first):
                place(keys, values, ref, 0, 0, first, here)
                place(keys, values, ref, UPPER, HALF, first, here)

        if back:
            first = first + jnp.where(z >= back, (here + TILE - 1) // TILE * TILE, 0)
    fill(keys, values, first + 2 * HALF, KEYS, 0.0)
    free = first // KEYS
    chunks = (first + jnp.minimum(before + count, 2 * HALF) + KEYS - 1) // KEYS

    def per_tile(tile, _):
        slots = pl.ds(pl.multiple_of(tile * QT, QT), QT)
        mine = [ref.at[tile] for ref in (top, lsum, acc)]
        mine[0][...] = jnp.full((4 * QT, HD), NEG, F32)
        mine[1][...] = jnp.zeros((4 * QT, HD), F32)
        mine[2][...] = jnp.zeros((4 * QT, HD), F32)
        query_pos = first + before + tile * QT + iota((4 * QT, 1), 0) % QT
        weigh = softmax_chunks(
            heads_of(q_ref, slots), query_pos, free, chunks, keys, values, scores, *mine
        )
        lax.fori_loop(0, chunks, weigh, 0)
        return 0

    lax.fori_loop(0, (count + QT - 1) // QT, per_tile, 0)


def attend_near(index, q, pieces):
    most = 5 * 2 * HALF + KEYS
    most = (most + KEYS - 1) // KEYS * KEYS
    return pl.pallas_call(
        attend_near_kernel,
        in_specs=[pl.BlockSpec(memory_space=pltpu.SMEM)] + [vmem()] * (1 + len(pieces)),
        out_specs=[vmem()] * 3 + [pl.BlockSpec(memory_space=pltpu.SMEM)],
        out_shape=[jax.ShapeDtypeStruct((CAP // QT, 4 * QT, HD), F32)] * 3
        + [jax.ShapeDtypeStruct((2,), jnp.int32)],
        scratch_shapes=[
            pltpu.VMEM((most, 2 * HD), BF),
            pltpu.VMEM((most, HD), BF),
            pltpu.VMEM((most // KEYS, 4 * QT, KEYS), F32),
        ],
        compiler_params=params(),
        cost_estimate=pl.CostEstimate(
            flops=12 * QT * most * 3 * HD * 2, bytes_accessed=1 << 23, transcendentals=8 * QT * most
        ),
        name="attend_near",
    )(index, q, *pieces)


def add_tile(tile, q_ref, given, mine, chunks, keys, values, scores):
    slots = pl.ds(pl.multiple_of(tile * QT, QT), QT)
    mine[0][...] = given[0][tile]
    weigh = softmax_chunks(
        heads_of(q_ref, slots), None, chunks, chunks, keys, values, scores, *mine
    )
    factor = jnp.exp2(given[0][tile] - mine[0][...])
    mine[1][...] = given[1][tile] * factor
    mine[2][...] = given[2][tile] * factor
    lax.fori_loop(0, chunks, weigh, 0)


def attend_more_kernel(index_ref, info_ref, q_ref, came, swapped, top, lsum, acc, *refs):
    results, out_info, (keys, values, scores) = refs[:3], refs[3], refs[4:]
    z, core = index_ref[0], index_ref[2]
    first, most = jnp.int32(0), info_ref[0]
    for back, where in ((5, (swapped, came)), (3, (came, swapped))):
        live = single(jnp.where(core == 0, table_of(where[0]), table_of(where[1])))
        most = jnp.maximum(most, live)
        here = jnp.minimum(live, 2 * HALF)
        for c in range(2):

            @pl.when((z >= back) & (core == c))
            def _(ref=where[c], here=here, first=first):
                place(keys, values, ref, 0, 0, first, here)
                place(keys, values, ref, UPPER, HALF, first, here)

        first = first + jnp.where(z >= back, (here + TILE - 1) // TILE * TILE, 0)
    fill(keys, values, first, KEYS, NEG)
    chunks = (first + KEYS - 1) // KEYS
    out_info[0] = most
    out_info[1] = info_ref[1]

    def per_tile(tile, _):
        mine = [ref.at[tile] for ref in results]
        add_tile(tile, q_ref, (top, lsum, acc), mine, chunks, keys, values, scores)
        return 0

    lax.fori_loop(0, (info_ref[1] + QT - 1) // QT, per_tile, 0)


def attend_more(index, q, came, swapped, state, info):
    most = 2 * 2 * HALF + KEYS
    most = (most + KEYS - 1) // KEYS * KEYS
    return pl.pallas_call(
        attend_more_kernel,
        in_specs=[pl.BlockSpec(memory_space=pltpu.SMEM)] * 2 + [vmem()] * 6,
        out_specs=[vmem()] * 3 + [pl.BlockSpec(memory_space=pltpu.SMEM)],
        out_shape=[jax.ShapeDtypeStruct(value.shape, F32) for value in state]
        + [jax.ShapeDtypeStruct((2,), jnp.int32)],
        scratch_shapes=[
            pltpu.VMEM((most, 2 * HD), BF),
            pltpu.VMEM((most, HD), BF),
            pltpu.VMEM((most // KEYS, 4 * QT, KEYS), F32),
        ],
        compiler_params=params(),
        cost_estimate=pl.CostEstimate(
            flops=12 * QT * most * 3 * HD * 2, bytes_accessed=1 << 23, transcendentals=8 * QT * most
        ),
        name="attend_more",
    )(index, info, q, came, swapped, *state)


def attend_far_kernel(index_ref, info_ref, q_ref, wout_ref, came, swapped, top, lsum, acc, *refs):
    outs, flag_ref = refs[:4], refs[4]
    keys, values, scores, peak, total, sums = refs[5:]
    z, core, y = index_ref[0], index_ref[2], index_ref[3]
    for out in outs:
        out[...] = jnp.zeros_like(out)
    live = single(table_of_far(came, core))
    flag_ref[0] = (jnp.maximum(info_ref[0], live) > 2 * HALF).astype(jnp.int32)
    count = info_ref[1]
    here = jnp.minimum(live, 2 * HALF)
    for c, lower, upper in ((0, came, swapped), (1, swapped, came)):

        @pl.when(core == c)
        def _(lower=lower, upper=upper):
            place(keys, values, lower, 0, 0, 0, here)
            place(keys, values, upper, TILE, HALF, 0, here)

    fill(keys, values, 2 * HALF, 2 * KEYS - 2 * HALF, NEG)
    chunks = jnp.where(z >= 4, (here + KEYS - 1) // KEYS, 0)

    def per_tile(tile, _):
        slots = pl.ds(pl.multiple_of(tile * QT, QT), QT)
        add_tile(
            tile, q_ref, (top, lsum, acc), (peak, total, sums), chunks, keys, values, scores
        )
        a = (sums[...] / jnp.sum(total[...], axis=1, keepdims=True)).astype(BF)
        a = jnp.concatenate([a[h * QT : (h + 1) * QT, :] for h in range(4)], axis=1)
        for k in range(4):
            cols = pl.ds(pl.multiple_of(((y + k) % 4) * 256, 256), 256)
            outs[k][slots, :] = jnp.dot(
                a, wout_ref[:, cols], preferred_element_type=F32
            ).astype(BF)
        return 0

    lax.fori_loop(0, (count + QT - 1) // QT, per_tile, 0)


def table_of_far(came, core):
    low, high = came[:TILE, :HD].astype(F32), came[HALF:UPPER, :HD].astype(F32)
    return jnp.where(core == 0, high, low)


def attend_far(index, info, q, wout, came, swapped, state):
    *parts, flag = pl.pallas_call(
        attend_far_kernel,
        in_specs=[pl.BlockSpec(memory_space=pltpu.SMEM)] * 2 + [vmem()] * 7,
        out_specs=[vmem()] * 4 + [pl.BlockSpec(memory_space=pltpu.SMEM)],
        out_shape=[jax.ShapeDtypeStruct((CAP, 256), BF)] * 4
        + [jax.ShapeDtypeStruct((1,), jnp.int32)],
        scratch_shapes=[
            pltpu.VMEM((2 * KEYS, 2 * HD), BF),
            pltpu.VMEM((2 * KEYS, HD), BF),
            pltpu.VMEM((2, 4 * QT, KEYS), F32),
        ]
        + [pltpu.VMEM((4 * QT, HD), F32)] * 3,
        compiler_params=params(),
        name="attend_far",
    )(index, info, q, wout, came, swapped, *state)
    return parts, flag[0]


def attend_any(kv, q, lengths, wout, y):
    device = lax.axis_index("seq")
    devices = lax.axis_size("seq")
    queries = q.reshape(CAP, 4, HD)
    slot = jnp.arange(CAP, dtype=jnp.int32)

    def step(turn, carry):
        block, top, total, weighted = carry
        source = (device - turn) % devices
        keys, values = block[:CAP, :HD], block[:CAP, HD:]
        live = block[CAP, 0].astype(jnp.int32)
        s = jnp.einsum("wgd,rd->wgr", queries, keys, preferred_element_type=F32)
        later = (source == device) & (slot[None, :] > slot[:, None])
        allowed = ((slot < live)[None, :] & (source <= device) & ~later)[:, None, :]
        s = jnp.where(allowed, s, NEG)
        new = jnp.maximum(top, jnp.max(s, axis=2))
        factor = jnp.exp2(top - new)
        w = jnp.where(allowed, jnp.exp2(s - new[..., None]), 0.0)
        total = total * factor + jnp.sum(w, axis=2)
        weighted = weighted * factor[..., None] + jnp.einsum(
            "wgr,rd->wgd", w.astype(BF), values, preferred_element_type=F32
        )
        block = lax.ppermute(block, "seq", [(i, (i + 1) % devices) for i in range(devices)])
        return block, new, total, weighted

    start = (
        kv,
        jnp.full((CAP, 4), NEG, F32),
        jnp.zeros((CAP, 4), F32),
        jnp.zeros((CAP, 4, HD), F32),
    )
    _, _, total, weighted = lax.fori_loop(0, devices, step, start)
    a = (weighted / total[..., None]).reshape(CAP, 4 * HD).astype(BF)
    part = jnp.dot(a, wout, preferred_element_type=F32).astype(BF)
    return [lax.dynamic_slice_in_dim(part, ((y + k) % 4) * 256, 256, 1) for k in range(4)]


def mix_kernel(len_ref, skip_ref, p0, p1, p2, p3, mixed_ref, tail_ref):
    byte_rows = skip_ref.shape[0]
    lengths = len_ref[...].astype(F32)
    inner = p0[...].astype(F32) + p1[...].astype(F32) + p2[...].astype(F32) + p3[...].astype(F32)
    i, j = iota((CAP, CAP), 0), iota((CAP, CAP), 1)
    column = jnp.sum(jnp.where(i == j, lengths, 0.0), axis=1, keepdims=True)
    start = jnp.sum(jnp.where(i < j, column, 0.0), axis=0, keepdims=True)
    at = iota((byte_rows, CAP), 0).astype(F32)
    hot = jnp.where((at >= start) & (at < start + lengths), 1.0, 0.0).astype(BF)
    up = jnp.dot(hot, inner.astype(BF), preferred_element_type=F32)
    mixed = (skip_ref[...].astype(F32) + up).astype(BF)
    mixed_ref[...] = mixed
    tail_ref[...] = mixed[byte_rows - HALO :, :]


def mix(lengths, skip, parts):
    return pl.pallas_call(
        mix_kernel,
        in_specs=[vmem()] * 6,
        out_specs=[vmem()] * 2,
        out_shape=[
            jax.ShapeDtypeStruct(skip.shape, BF),
            jax.ShapeDtypeStruct((HALO, skip.shape[1]), BF),
        ],
        compiler_params=params(),
        name="mix",
    )(lengths, skip, *parts)


def filtered(window, taps):
    rows = window.shape[0] - HALO
    total = jnp.zeros((rows, window.shape[1]), F32)
    lags = taps.shape[0]
    for r in range(8):
        moved = window[8 - r : rows + HALO - r, :]
        for lag in range(r, lags, 8):
            low = HALO - 8 - (lag - r)
            total += taps[lag : lag + 1, :] * moved[low : low + rows, :]
    return (window[HALO:, :] + total / (1.0 + jnp.exp(-total))).astype(BF)


def conv_kernel(mixed_ref, taps_ref, out_ref, ext):
    byte_rows, channels = mixed_ref.shape
    ext[:HALO, :] = jnp.zeros((HALO, channels), F32)
    ext[HALO:, :] = mixed_ref[...].astype(F32)
    block = 64

    def per_block(i, _):
        first = pl.multiple_of(i * block, block)
        for low in range(0, channels, 128):
            part = slice(low, low + 128)
            window = ext[pl.ds(first, block + HALO), part]
            out_ref[pl.ds(first, block), part] = filtered(window, taps_ref[:, part])
        return 0

    lax.fori_loop(0, byte_rows // block, per_block, 0)


def rim_kernel(given_hbm, rim_ref, mixed_ref, taps_ref, out_hbm, rows, sem):
    del given_hbm
    for low in range(0, mixed_ref.shape[1], 128):
        part = slice(low, low + 128)
        window = jnp.concatenate([rim_ref[:, part], mixed_ref[:HALO, part]], axis=0).astype(F32)
        rows[:, part] = filtered(window, taps_ref[:, part])
    copy = pltpu.make_async_copy(rows, out_hbm.at[pl.ds(0, HALO)], sem)
    copy.start()
    copy.wait()


def convolve(mixed, taps):
    return pl.pallas_call(
        conv_kernel,
        in_specs=[vmem()] * 2,
        out_specs=vmem(),
        out_shape=jax.ShapeDtypeStruct(mixed.shape, BF),
        scratch_shapes=[pltpu.VMEM((HALO + mixed.shape[0], mixed.shape[1]), F32)],
        compiler_params=params(),
        cost_estimate=pl.CostEstimate(
            flops=2 * mixed.size * taps.shape[0], bytes_accessed=16 * mixed.size, transcendentals=0
        ),
        name="convolve",
    )(mixed, taps)


def first_rows(given, rim, mixed, taps):
    return pl.pallas_call(
        rim_kernel,
        in_specs=[anywhere()] + [vmem()] * 3,
        out_specs=anywhere(),
        out_shape=jax.ShapeDtypeStruct(given.shape, BF),
        input_output_aliases={0: 0},
        scratch_shapes=[pltpu.VMEM((HALO, mixed.shape[1]), BF), pltpu.SemaphoreType.DMA],
        compiler_params=params(),
        name="first_rows",
    )(given, rim, mixed, taps)


def seq_permute(value, move):
    pairs = []
    for z in range(NZ):
        for x in range(NX):
            for core in range(2):
                tz, tx, tc = move(z, x, core)
                target = ((tz % NZ) * NX + tx % NX) * 2 + tc
                pairs.append(((z * NX + x) * 2 + core, target))
    return lax.ppermute(value, "seq", pairs)


def along_x(value, steps):
    return seq_permute(value, lambda z, x, c: (z, x + steps, c))


def round_z(value):
    return seq_permute(value, lambda z, x, c: (z + 1 - 2 * c, x, c))


def swap(value):
    return seq_permute(value, lambda z, x, c: (z, x, 1 - c))


def per_device(enc, span_len, skip, gain, wq, wk, wv, wout, taps):
    seq = lax.axis_index("seq")
    y = lax.axis_index("section")
    index = jnp.stack([seq // (2 * NX), (seq // 2) % NX, seq % 2, y]).astype(jnp.int32)
    kv, x, scale = pool(span_len, enc, gain.reshape(1, -1), wk, wv)
    column = [kv, along_x(kv, 1), along_x(kv, -1), along_x(kv, 2)]
    plane = compact(index, column + [swap(v) for v in column])
    first, q = lax.optimization_barrier((round_z(plane), query(x, wq, scale)))
    came = [first]
    came.append(round_z(first))
    near = attend_near(index, q, [plane] + came + [swap(piece) for piece in came])
    third, (*state, info) = lax.optimization_barrier((round_z(came[-1]), near))
    far = round_z(lax.dynamic_slice_in_dim(third, (seq % 2) * HALF, UPPER, 0))
    more = attend_more(index, q, third, swap(third), state, info)
    far, (*state, info) = lax.optimization_barrier((far, more))
    parts, crowded = attend_far(index, info, q, wout, far, swap(far), state)
    parts = lax.cond(
        crowded > 0, lambda _: attend_any(kv, q, span_len, wout, y), lambda given: given, parts
    )
    sent = [
        lax.ppermute(parts[k], "section", [(i, (i + k) % 4) for i in range(4)]) for k in (1, 2, 3)
    ]
    mixed, tail = mix(span_len, skip, [parts[0]] + sent)
    rim = lax.ppermute(tail, "seq", [(i, i + 1) for i in range(2 * NX * NZ - 1)])
    return first_rows(convolve(mixed, taps), rim, mixed, taps)


def solution(mesh):
    return jax.shard_map(
        per_device,
        mesh=mesh,
        in_specs=(
            P("seq", None),
            P("seq", None),
            P("seq", "section"),
            P(),
            P(None, "section"),
            P(None, "section"),
            P(None, "section"),
            P("section", None),
            P(None, "section"),
        ),
        out_specs=P("seq", "section"),
        check_vma=False,
    )
```

```python
import math

import jax
import jax.numpy as jnp
from jax import lax
from jax.experimental import pallas as pl
from jax.experimental.pallas import tpu as pltpu
from jax.sharding import PartitionSpec as P

HD = 128
CAP = 192
TILE = 16
ROWS = CAP + TILE
NX = 4
NZ = 8
HALF = 352
UPPER = HALF + TILE
PIECE = UPPER + HALF
QT = 96
KEYS = 512
POOL_STEPS = 4
DEPTH = 4
FULL = 62
QUERY_LIMIT = 60
HALO = 32
LOG2E = math.log2(math.e)
NEG = -1e30
MIB = 1 << 20
BF = jnp.bfloat16
F32 = jnp.float32


def vmem():
    return pl.BlockSpec(memory_space=pltpu.VMEM)


def anywhere():
    return pl.BlockSpec(memory_space=pl.ANY)


def params(limit=48):
    return pltpu.CompilerParams(vmem_limit_bytes=limit * MIB)


def iota(shape, dim):
    return lax.broadcasted_iota(jnp.int32, shape, dim)


def pool_kernel(len_hbm, gain_hbm, enc_hbm, wk_hbm, wv_hbm, kv_ref, x_ref, scale_ref, lengths, gain, enc, wkv, sems):
    byte_rows, width = enc.shape
    block = width // POOL_STEPS
    small = [
        pltpu.make_async_copy(len_hbm, lengths, sems.at[0]),
        pltpu.make_async_copy(gain_hbm, gain, sems.at[1]),
    ]
    for copy in small:
        copy.start()
    copies = []
    for step in range(POOL_STEPS):
        part = pl.ds(step * block, block)
        at = 2 + 3 * step
        group = [
            pltpu.make_async_copy(enc_hbm.at[:, part], enc.at[:, part], sems.at[at]),
            pltpu.make_async_copy(wk_hbm.at[part], wkv.at[part, pl.ds(0, HD)], sems.at[at + 1]),
            pltpu.make_async_copy(wv_hbm.at[part], wkv.at[part, pl.ds(HD, HD)], sems.at[at + 2]),
        ]
        copies.append(group)
        if step < DEPTH:
            for copy in group:
                copy.start()
    for copy in small:
        copy.wait()
    before = iota((CAP, CAP), 1) < iota((CAP, CAP), 0)
    start = jnp.sum(jnp.where(before, lengths[...], 0).astype(F32), axis=1, keepdims=True)
    hot = jnp.where(iota((CAP, byte_rows), 1).astype(F32) == start, 1.0, 0.0).astype(BF)
    total = jnp.zeros((CAP, 2 * HD), F32)
    squares = jnp.zeros((CAP, HD), F32)
    held = None
    for step in range(POOL_STEPS + 1):
        if step < POOL_STEPS:
            for copy in copies[step]:
                copy.wait()
            if step + DEPTH < POOL_STEPS:
                for copy in copies[step + DEPTH]:
                    copy.start()
        if held is not None:
            last = slice((step - 1) * block, step * block)
            total += jnp.dot(held, wkv[last, :], preferred_element_type=F32)
        if step < POOL_STEPS:
            part = slice(step * block, (step + 1) * block)
            pooled = jnp.dot(hot, enc[:, part], preferred_element_type=F32)
            for k in range(block // HD):
                piece = pooled[:, k * HD : (k + 1) * HD]
                squares += piece * piece
            held = (pooled * gain[:, part]).astype(BF)
            x_ref[:, part] = held
    scale = lax.rsqrt(jnp.sum(squares, axis=1, keepdims=True) / width + 1e-5)
    scale_ref[...] = jnp.broadcast_to(scale, scale_ref.shape)
    kv_ref[:CAP, :] = (total * scale).astype(BF)
    count = jnp.sum((lengths[...] > 0).astype(F32), axis=1, keepdims=True)
    kv_ref[CAP:, :] = jnp.broadcast_to(count, (TILE, 2 * HD)).astype(BF)


def pool(lengths, enc, gain, wk, wv):
    byte_rows, width = enc.shape
    return pl.pallas_call(
        pool_kernel,
        in_specs=[anywhere()] * 5,
        out_specs=[vmem()] * 3,
        out_shape=[
            jax.ShapeDtypeStruct((ROWS, 2 * HD), BF),
            jax.ShapeDtypeStruct((CAP, width), BF),
            jax.ShapeDtypeStruct((CAP, HD), F32),
        ],
        scratch_shapes=[
            pltpu.VMEM(lengths.shape, jnp.int32),
            pltpu.VMEM(gain.shape, F32),
            pltpu.VMEM((byte_rows, width), BF),
            pltpu.VMEM((width, 2 * HD), BF),
            pltpu.SemaphoreType.DMA((3 * POOL_STEPS + 2,)),
        ],
        compiler_params=params(FULL),
        cost_estimate=pl.CostEstimate(
            flops=2 * CAP * width * (byte_rows + 2 * HD),
            bytes_accessed=2 * width * (byte_rows + CAP + 2 * HD),
            transcendentals=0,
        ),
        name="pool",
    )(lengths, gain, enc, wk, wv)


def query_kernel(x_ref, scale_ref, wq_hbm, q_ref, wq, sems):
    width = wq.shape[0]
    block = width // POOL_STEPS
    copies = []
    for step in range(POOL_STEPS):
        part = pl.ds(step * block, block)
        copies.append(pltpu.make_async_copy(wq_hbm.at[part], wq.at[part], sems.at[step]))
        copies[-1].start()
    total = jnp.zeros(q_ref.shape, F32)
    for step in range(POOL_STEPS):
        copies[step].wait()
        part = slice(step * block, (step + 1) * block)
        total += jnp.dot(x_ref[:, part], wq[part, :], preferred_element_type=F32)
    q_ref[...] = (total * (scale_ref[:, :1] * (LOG2E * HD**-0.5))).astype(BF)


def query(x, wq, scale):
    width, out = wq.shape
    return pl.pallas_call(
        query_kernel,
        in_specs=[vmem(), vmem(), anywhere()],
        out_specs=vmem(),
        out_shape=jax.ShapeDtypeStruct((CAP, out), BF),
        scratch_shapes=[
            pltpu.VMEM((width, out), BF),
            pltpu.SemaphoreType.DMA((POOL_STEPS,)),
        ],
        compiler_params=params(QUERY_LIMIT),
        cost_estimate=pl.CostEstimate(
            flops=2 * CAP * width * out, bytes_accessed=2 * width * (out + CAP), transcendentals=0
        ),
        name="query",
    )(x, scale, wq)


def compact_kernel(index_ref, *refs):
    blocks, out_ref = refs[:8], refs[8]
    x, core = index_ref[1], index_ref[2]
    shifts = (0, 1, 3, 2)
    order = [
        ((x + NX - shift) % NX) * 2 + (core if side == 0 else 1 - core)
        for side in range(2)
        for shift in shifts
    ]
    counts = [ref[CAP : CAP + TILE, :].astype(F32)[:1, :] for ref in blocks]
    lane = iota((1, CAP), 1).astype(F32)
    targets = []
    for i in range(8):
        first = jnp.zeros((1, 2 * HD), F32)
        for k in range(8):
            if k != i:
                first += jnp.where(order[k] < order[i], counts[k], 0.0)
        targets.append(jnp.where(lane < counts[i][:, :CAP], first[:, :CAP] + lane, -1.0))
    sub = iota((TILE, 2 * HD), 0)
    table = jnp.zeros((TILE, 2 * HD), F32)
    for i in range(8):
        table += jnp.where(sub == order[i], counts[i], 0.0)
    out_ref[HALF:UPPER, :] = table.astype(BF)
    for half in range(2):
        row = (iota((HALF, CAP), 0) + half * HALF).astype(F32)
        total = jnp.zeros((HALF, 2 * HD), F32)
        for i in range(8):
            hot = jnp.where(row == targets[i], 1.0, 0.0).astype(BF)
            total += jnp.dot(hot, blocks[i][:CAP, :], preferred_element_type=F32)
        out_ref[half * UPPER : half * UPPER + HALF, :] = total.astype(BF)


def compact(index, blocks):
    return pl.pallas_call(
        compact_kernel,
        in_specs=[pl.BlockSpec(memory_space=pltpu.SMEM)] + [vmem()] * 8,
        out_specs=vmem(),
        out_shape=jax.ShapeDtypeStruct((PIECE, 2 * HD), BF),
        compiler_params=params(),
        name="compact",
    )(index, *blocks)


def single(value):
    return jnp.max(jnp.sum(value, axis=0, keepdims=True)).astype(jnp.int32)


def table_of(ref):
    return ref[HALF:UPPER, :HD].astype(F32)


def heads_of(q_ref, slots):
    q = jnp.concatenate([q_ref[slots, h * HD : (h + 1) * HD] for h in range(4)], axis=0)
    ones = jnp.where(iota((4 * QT, HD), 1) == 0, 1.0, 0.0).astype(BF)
    return jnp.concatenate([q, ones], axis=1)


def place(keys, values, ref, low, to_row, first, live):
    to = pl.ds(pl.multiple_of(first + to_row, TILE), HALF)
    keys[to, :HD] = ref[low : low + HALF, :HD]
    values[to, :] = ref[low : low + HALF, HD:]
    dead = jnp.where(iota((HALF, HD), 0) + to_row < live, 0.0, NEG)
    keys[to, HD:] = dead.astype(BF)


def fill(keys, values, start, rows, bias):
    end = pl.ds(pl.multiple_of(start, TILE), rows)
    keys[end, :HD] = jnp.zeros((rows, HD), BF)
    keys[end, HD:] = jnp.full((rows, HD), bias, BF)
    values[end, :] = jnp.zeros((rows, HD), BF)


def softmax_chunks(q, query_pos, free, chunks, keys, values, scores, top, lsum, acc):
    def score(c):
        rows = pl.ds(pl.multiple_of(c * KEYS, KEYS), KEYS)
        return lax.dot_general(
            q, keys[rows, :], (((1,), (1,)), ((), ())), preferred_element_type=F32
        )

    def keep(c, s):
        scores[c] = s
        best = top[...]
        for k in range(KEYS // HD):
            best = jnp.maximum(best, s[:, k * HD : (k + 1) * HD])
        top[...] = best

    def open_chunk(c, _):
        keep(c, score(c))
        return 0

    def masked_chunk(c, _):
        allowed = c * KEYS + iota((4 * QT, KEYS), 1) <= query_pos
        keep(c, jnp.where(allowed, score(c), NEG))
        return 0

    lax.fori_loop(0, free, open_chunk, 0)
    if query_pos is not None:
        lax.fori_loop(free, chunks, masked_chunk, 0)
    top[...] = jnp.broadcast_to(jnp.max(top[...], axis=1, keepdims=True), top.shape)

    def weigh(c, _):
        best = top[...]
        parts = [jnp.exp2(scores[c, :, k * HD : (k + 1) * HD] - best) for k in range(KEYS // HD)]
        total = parts[0]
        for part in parts[1:]:
            total = total + part
        lsum[...] += total
        p = jnp.concatenate([part.astype(BF) for part in parts], axis=1)
        rows = pl.ds(pl.multiple_of(c * KEYS, KEYS), KEYS)
        acc[...] += jnp.dot(p, values[rows, :], preferred_element_type=F32)
        return 0

    return weigh


def attend_near_kernel(index_ref, q_ref, *refs):
    pieces, (top, lsum, acc, info_ref) = refs[:5], refs[5:9]
    keys, values, scores = refs[9:]
    z, x, core = index_ref[0], index_ref[1], index_ref[2]
    own = x * 2 + core

    own_piece, came, swapped = pieces[0], pieces[1:3], pieces[3:5]
    upward, downward = (came, swapped), (swapped, came)
    planes = [(8 - s, [downward[c][s - 1] for c in range(2)]) for s in (1, 2)]
    planes += [(s, [upward[c][s - 1] for c in range(2)]) for s in (2, 1)]
    planes.append((0, [own_piece, own_piece]))

    lives, most = [], jnp.int32(0)
    for back, (a, b) in planes:
        table = jnp.where(core == 0, table_of(a), table_of(b)) if back else table_of(a)
        lives.append(single(table))
        most = jnp.maximum(most, lives[-1])
    row = iota((TILE, HD), 0)
    own_table = table_of(own_piece)
    before = single(jnp.where(row < own, own_table, 0.0))
    count = single(jnp.where(row == own, own_table, 0.0))
    info_ref[0] = most
    info_ref[1] = count

    first = jnp.int32(0)
    for (back, where), live in zip(planes, lives):
        here = jnp.minimum(live, 2 * HALF)
        for c in range(2 if back else 1):
            wanted = (z >= back) & (core == c) if back else z >= 0

            @pl.when(wanted)
            def _(ref=where[c], here=here, first=first):
                place(keys, values, ref, 0, 0, first, here)
                place(keys, values, ref, UPPER, HALF, first, here)

        if back:
            first = first + jnp.where(z >= back, (here + TILE - 1) // TILE * TILE, 0)
    fill(keys, values, first + 2 * HALF, KEYS, 0.0)
    free = first // KEYS
    chunks = (first + jnp.minimum(before + count, 2 * HALF) + KEYS - 1) // KEYS

    def per_tile(tile, _):
        slots = pl.ds(pl.multiple_of(tile * QT, QT), QT)
        mine = [ref.at[tile] for ref in (top, lsum, acc)]
        mine[0][...] = jnp.full((4 * QT, HD), NEG, F32)
        mine[1][...] = jnp.zeros((4 * QT, HD), F32)
        mine[2][...] = jnp.zeros((4 * QT, HD), F32)
        query_pos = first + before + tile * QT + iota((4 * QT, 1), 0) % QT
        weigh = softmax_chunks(
            heads_of(q_ref, slots), query_pos, free, chunks, keys, values, scores, *mine
        )
        lax.fori_loop(0, chunks, weigh, 0)
        return 0

    lax.fori_loop(0, (count + QT - 1) // QT, per_tile, 0)


def attend_near(index, q, pieces):
    most = 5 * 2 * HALF + KEYS
    most = (most + KEYS - 1) // KEYS * KEYS
    return pl.pallas_call(
        attend_near_kernel,
        in_specs=[pl.BlockSpec(memory_space=pltpu.SMEM)] + [vmem()] * (1 + len(pieces)),
        out_specs=[vmem()] * 3 + [pl.BlockSpec(memory_space=pltpu.SMEM)],
        out_shape=[jax.ShapeDtypeStruct((CAP // QT, 4 * QT, HD), F32)] * 3
        + [jax.ShapeDtypeStruct((2,), jnp.int32)],
        scratch_shapes=[
            pltpu.VMEM((most, 2 * HD), BF),
            pltpu.VMEM((most, HD), BF),
            pltpu.VMEM((most // KEYS, 4 * QT, KEYS), F32),
        ],
        compiler_params=params(),
        cost_estimate=pl.CostEstimate(
            flops=12 * QT * most * 3 * HD * 2, bytes_accessed=1 << 23, transcendentals=8 * QT * most
        ),
        name="attend_near",
    )(index, q, *pieces)


def add_tile(tile, q_ref, given, mine, chunks, keys, values, scores):
    slots = pl.ds(pl.multiple_of(tile * QT, QT), QT)
    mine[0][...] = given[0][tile]
    weigh = softmax_chunks(
        heads_of(q_ref, slots), None, chunks, chunks, keys, values, scores, *mine
    )
    factor = jnp.exp2(given[0][tile] - mine[0][...])
    mine[1][...] = given[1][tile] * factor
    mine[2][...] = given[2][tile] * factor
    lax.fori_loop(0, chunks, weigh, 0)


def attend_more_kernel(index_ref, info_ref, q_ref, came, swapped, top, lsum, acc, *refs):
    results, out_info, (keys, values, scores) = refs[:3], refs[3], refs[4:]
    z, core = index_ref[0], index_ref[2]
    first, most = jnp.int32(0), info_ref[0]
    for back, where in ((5, (swapped, came)), (3, (came, swapped))):
        live = single(jnp.where(core == 0, table_of(where[0]), table_of(where[1])))
        most = jnp.maximum(most, live)
        here = jnp.minimum(live, 2 * HALF)
        for c in range(2):

            @pl.when((z >= back) & (core == c))
            def _(ref=where[c], here=here, first=first):
                place(keys, values, ref, 0, 0, first, here)
                place(keys, values, ref, UPPER, HALF, first, here)

        first = first + jnp.where(z >= back, (here + TILE - 1) // TILE * TILE, 0)
    fill(keys, values, first, KEYS, NEG)
    chunks = (first + KEYS - 1) // KEYS
    out_info[0] = most
    out_info[1] = info_ref[1]

    def per_tile(tile, _):
        mine = [ref.at[tile] for ref in results]
        add_tile(tile, q_ref, (top, lsum, acc), mine, chunks, keys, values, scores)
        return 0

    lax.fori_loop(0, (info_ref[1] + QT - 1) // QT, per_tile, 0)


def attend_more(index, q, came, swapped, state, info):
    most = 2 * 2 * HALF + KEYS
    most = (most + KEYS - 1) // KEYS * KEYS
    return pl.pallas_call(
        attend_more_kernel,
        in_specs=[pl.BlockSpec(memory_space=pltpu.SMEM)] * 2 + [vmem()] * 6,
        out_specs=[vmem()] * 3 + [pl.BlockSpec(memory_space=pltpu.SMEM)],
        out_shape=[jax.ShapeDtypeStruct(value.shape, F32) for value in state]
        + [jax.ShapeDtypeStruct((2,), jnp.int32)],
        scratch_shapes=[
            pltpu.VMEM((most, 2 * HD), BF),
            pltpu.VMEM((most, HD), BF),
            pltpu.VMEM((most // KEYS, 4 * QT, KEYS), F32),
        ],
        compiler_params=params(),
        cost_estimate=pl.CostEstimate(
            flops=12 * QT * most * 3 * HD * 2, bytes_accessed=1 << 23, transcendentals=8 * QT * most
        ),
        name="attend_more",
    )(index, info, q, came, swapped, *state)


def attend_far_kernel(index_ref, info_ref, q_ref, wout_ref, came, swapped, top, lsum, acc, *refs):
    outs, flag_ref = refs[:4], refs[4]
    keys, values, scores, peak, total, sums = refs[5:]
    z, core, y = index_ref[0], index_ref[2], index_ref[3]
    for out in outs:
        out[...] = jnp.zeros_like(out)
    live = single(table_of_far(came, core))
    flag_ref[0] = (jnp.maximum(info_ref[0], live) > 2 * HALF).astype(jnp.int32)
    count = info_ref[1]
    here = jnp.minimum(live, 2 * HALF)
    for c, lower, upper in ((0, came, swapped), (1, swapped, came)):

        @pl.when(core == c)
        def _(lower=lower, upper=upper):
            place(keys, values, lower, 0, 0, 0, here)
            place(keys, values, upper, TILE, HALF, 0, here)

    fill(keys, values, 2 * HALF, 2 * KEYS - 2 * HALF, NEG)
    chunks = jnp.where(z >= 4, (here + KEYS - 1) // KEYS, 0)

    def per_tile(tile, _):
        slots = pl.ds(pl.multiple_of(tile * QT, QT), QT)
        add_tile(
            tile, q_ref, (top, lsum, acc), (peak, total, sums), chunks, keys, values, scores
        )
        a = (sums[...] / jnp.sum(total[...], axis=1, keepdims=True)).astype(BF)
        a = jnp.concatenate([a[h * QT : (h + 1) * QT, :] for h in range(4)], axis=1)
        for k in range(4):
            cols = pl.ds(pl.multiple_of(((y + k) % 4) * 256, 256), 256)
            outs[k][slots, :] = jnp.dot(
                a, wout_ref[:, cols], preferred_element_type=F32
            ).astype(BF)
        return 0

    lax.fori_loop(0, (count + QT - 1) // QT, per_tile, 0)


def table_of_far(came, core):
    low, high = came[:TILE, :HD].astype(F32), came[HALF:UPPER, :HD].astype(F32)
    return jnp.where(core == 0, high, low)


def attend_far(index, info, q, wout, came, swapped, state):
    *parts, flag = pl.pallas_call(
        attend_far_kernel,
        in_specs=[pl.BlockSpec(memory_space=pltpu.SMEM)] * 2 + [vmem()] * 7,
        out_specs=[vmem()] * 4 + [pl.BlockSpec(memory_space=pltpu.SMEM)],
        out_shape=[jax.ShapeDtypeStruct((CAP, 256), BF)] * 4
        + [jax.ShapeDtypeStruct((1,), jnp.int32)],
        scratch_shapes=[
            pltpu.VMEM((2 * KEYS, 2 * HD), BF),
            pltpu.VMEM((2 * KEYS, HD), BF),
            pltpu.VMEM((2, 4 * QT, KEYS), F32),
        ]
        + [pltpu.VMEM((4 * QT, HD), F32)] * 3,
        compiler_params=params(),
        name="attend_far",
    )(index, info, q, wout, came, swapped, *state)
    return parts, flag[0]


def attend_any(kv, q, lengths, wout, y):
    device = lax.axis_index("seq")
    devices = lax.axis_size("seq")
    queries = q.reshape(CAP, 4, HD)
    slot = jnp.arange(CAP, dtype=jnp.int32)

    def step(turn, carry):
        block, top, total, weighted = carry
        source = (device - turn) % devices
        keys, values = block[:CAP, :HD], block[:CAP, HD:]
        live = block[CAP, 0].astype(jnp.int32)
        s = jnp.einsum("wgd,rd->wgr", queries, keys, preferred_element_type=F32)
        later = (source == device) & (slot[None, :] > slot[:, None])
        allowed = ((slot < live)[None, :] & (source <= device) & ~later)[:, None, :]
        s = jnp.where(allowed, s, NEG)
        new = jnp.maximum(top, jnp.max(s, axis=2))
        factor = jnp.exp2(top - new)
        w = jnp.where(allowed, jnp.exp2(s - new[..., None]), 0.0)
        total = total * factor + jnp.sum(w, axis=2)
        weighted = weighted * factor[..., None] + jnp.einsum(
            "wgr,rd->wgd", w.astype(BF), values, preferred_element_type=F32
        )
        block = lax.ppermute(block, "seq", [(i, (i + 1) % devices) for i in range(devices)])
        return block, new, total, weighted

    start = (
        kv,
        jnp.full((CAP, 4), NEG, F32),
        jnp.zeros((CAP, 4), F32),
        jnp.zeros((CAP, 4, HD), F32),
    )
    _, _, total, weighted = lax.fori_loop(0, devices, step, start)
    a = (weighted / total[..., None]).reshape(CAP, 4 * HD).astype(BF)
    part = jnp.dot(a, wout, preferred_element_type=F32).astype(BF)
    return [lax.dynamic_slice_in_dim(part, ((y + k) % 4) * 256, 256, 1) for k in range(4)]


def mix_kernel(len_ref, skip_ref, p0, p1, p2, p3, mixed_ref, tail_ref):
    byte_rows = skip_ref.shape[0]
    lengths = len_ref[...].astype(F32)
    inner = p0[...].astype(F32) + p1[...].astype(F32) + p2[...].astype(F32) + p3[...].astype(F32)
    i, j = iota((CAP, CAP), 0), iota((CAP, CAP), 1)
    column = jnp.sum(jnp.where(i == j, lengths, 0.0), axis=1, keepdims=True)
    start = jnp.sum(jnp.where(i < j, column, 0.0), axis=0, keepdims=True)
    at = iota((byte_rows, CAP), 0).astype(F32)
    hot = jnp.where((at >= start) & (at < start + lengths), 1.0, 0.0).astype(BF)
    up = jnp.dot(hot, inner.astype(BF), preferred_element_type=F32)
    mixed = (skip_ref[...].astype(F32) + up).astype(BF)
    mixed_ref[...] = mixed
    tail_ref[...] = mixed[byte_rows - HALO :, :]


def mix(lengths, skip, parts):
    return pl.pallas_call(
        mix_kernel,
        in_specs=[vmem()] * 6,
        out_specs=[vmem()] * 2,
        out_shape=[
            jax.ShapeDtypeStruct(skip.shape, BF),
            jax.ShapeDtypeStruct((HALO, skip.shape[1]), BF),
        ],
        compiler_params=params(),
        name="mix",
    )(lengths, skip, *parts)


def filtered(window, taps):
    rows = window.shape[0] - HALO
    total = jnp.zeros((rows, window.shape[1]), F32)
    lags = taps.shape[0]
    for r in range(8):
        moved = window[8 - r : rows + HALO - r, :]
        for lag in range(r, lags, 8):
            low = HALO - 8 - (lag - r)
            total += taps[lag : lag + 1, :] * moved[low : low + rows, :]
    return (window[HALO:, :] + total / (1.0 + jnp.exp(-total))).astype(BF)


def conv_kernel(mixed_ref, taps_ref, out_ref, ext):
    byte_rows, channels = mixed_ref.shape
    ext[:HALO, :] = jnp.zeros((HALO, channels), F32)
    ext[HALO:, :] = mixed_ref[...].astype(F32)
    block = 128
    lags = taps_ref.shape[0]

    for first in range(0, byte_rows, block):
        for low in range(0, channels, 128):
            part = slice(low, low + 128)
            total = jnp.zeros((block, 128), F32)
            for lag in range(lags):
                start = first + HALO - lag
                total += taps_ref[lag : lag + 1, part] * ext[start : start + block, part]
            here = ext[first + HALO : first + HALO + block, part]
            silu = total / (1.0 + jnp.exp(-total))
            out_ref[first : first + block, part] = (here + silu).astype(BF)


def rim_kernel(given_hbm, rim_ref, mixed_ref, taps_ref, out_hbm, rows, sem):
    del given_hbm
    for low in range(0, mixed_ref.shape[1], 128):
        part = slice(low, low + 128)
        window = jnp.concatenate([rim_ref[:, part], mixed_ref[:HALO, part]], axis=0).astype(F32)
        rows[:, part] = filtered(window, taps_ref[:, part])
    copy = pltpu.make_async_copy(rows, out_hbm.at[pl.ds(0, HALO)], sem)
    copy.start()
    copy.wait()


def convolve(mixed, taps):
    return pl.pallas_call(
        conv_kernel,
        in_specs=[vmem()] * 2,
        out_specs=vmem(),
        out_shape=jax.ShapeDtypeStruct(mixed.shape, BF),
        scratch_shapes=[pltpu.VMEM((HALO + mixed.shape[0], mixed.shape[1]), F32)],
        compiler_params=params(),
        cost_estimate=pl.CostEstimate(
            flops=2 * mixed.size * taps.shape[0], bytes_accessed=16 * mixed.size, transcendentals=0
        ),
        name="convolve",
    )(mixed, taps)


def first_rows(given, rim, mixed, taps):
    return pl.pallas_call(
        rim_kernel,
        in_specs=[anywhere()] + [vmem()] * 3,
        out_specs=anywhere(),
        out_shape=jax.ShapeDtypeStruct(given.shape, BF),
        input_output_aliases={0: 0},
        scratch_shapes=[pltpu.VMEM((HALO, mixed.shape[1]), BF), pltpu.SemaphoreType.DMA],
        compiler_params=params(),
        name="first_rows",
    )(given, rim, mixed, taps)


def seq_permute(value, move):
    pairs = []
    for z in range(NZ):
        for x in range(NX):
            for core in range(2):
                tz, tx, tc = move(z, x, core)
                target = ((tz % NZ) * NX + tx % NX) * 2 + tc
                pairs.append(((z * NX + x) * 2 + core, target))
    return lax.ppermute(value, "seq", pairs)


def along_x(value, steps):
    return seq_permute(value, lambda z, x, c: (z, x + steps, c))


def round_z(value):
    return seq_permute(value, lambda z, x, c: (z + 1 - 2 * c, x, c))


def swap(value):
    return seq_permute(value, lambda z, x, c: (z, x, 1 - c))


def per_device(enc, span_len, skip, gain, wq, wk, wv, wout, taps):
    seq = lax.axis_index("seq")
    y = lax.axis_index("section")
    index = jnp.stack([seq // (2 * NX), (seq // 2) % NX, seq % 2, y]).astype(jnp.int32)
    kv, x, scale = pool(span_len, enc, gain.reshape(1, -1), wk, wv)
    across = along_x(kv, 2)
    column = [kv, along_x(kv, 1), along_x(kv, -1), across]
    plane = compact(index, column + [swap(v) for v in column])
    first, q = lax.optimization_barrier((round_z(plane), query(x, wq, scale)))
    came = [first]
    came.append(round_z(first))
    near = attend_near(index, q, [plane] + came + [swap(piece) for piece in came])
    third, (*state, info) = lax.optimization_barrier((round_z(came[-1]), near))
    far = round_z(lax.dynamic_slice_in_dim(third, (seq % 2) * HALF, UPPER, 0))
    more = attend_more(index, q, third, swap(third), state, info)
    far, (*state, info) = lax.optimization_barrier((far, more))
    parts, crowded = attend_far(index, info, q, wout, far, swap(far), state)
    parts = lax.cond(
        crowded > 0, lambda _: attend_any(kv, q, span_len, wout, y), lambda given: given, parts
    )
    sent = [
        lax.ppermute(parts[k], "section", [(i, (i + k) % 4) for i in range(4)]) for k in (2, 1, 3)
    ]
    mixed, tail = mix(span_len, skip, [parts[0]] + sent)
    rim = lax.ppermute(tail, "seq", [(i, i + 1) for i in range(2 * NX * NZ - 1)])
    return first_rows(convolve(mixed, taps), rim, mixed, taps)


def solution(mesh):
    return jax.shard_map(
        per_device,
        mesh=mesh,
        in_specs=(
            P("seq", None),
            P("seq", None),
            P("seq", "section"),
            P(),
            P(None, "section"),
            P(None, "section"),
            P(None, "section"),
            P("section", None),
            P(None, "section"),
        ),
        out_specs=P("seq", "section"),
        check_vma=False,
    )
```

```python
import math

import jax
import jax.numpy as jnp
from jax import lax
from jax.experimental import pallas as pl
from jax.experimental.pallas import tpu as pltpu
from jax.sharding import PartitionSpec as P

HD = 128
CAP = 192
TILE = 16
ROWS = CAP + TILE
NX = 4
NZ = 8
HALF = 352
UPPER = HALF + TILE
PIECE = UPPER + HALF
QT = 96
KEYS = 512
POOL_STEPS = 8
DEPTH = 8
FULL = 62
QUERY_LIMIT = 60
HALO = 32
LOG2E = math.log2(math.e)
NEG = -1e30
MIB = 1 << 20
BF = jnp.bfloat16
F32 = jnp.float32


def vmem():
    return pl.BlockSpec(memory_space=pltpu.VMEM)


def anywhere():
    return pl.BlockSpec(memory_space=pl.ANY)


def params(limit=48):
    return pltpu.CompilerParams(vmem_limit_bytes=limit * MIB)


def iota(shape, dim):
    return lax.broadcasted_iota(jnp.int32, shape, dim)


def pool_kernel(len_hbm, gain_hbm, enc_hbm, wk_hbm, wv_hbm, kv_ref, x_ref, scale_ref, lengths, gain, enc, wkv, sems):
    byte_rows, width = enc.shape
    block = width // POOL_STEPS
    small = [
        pltpu.make_async_copy(len_hbm, lengths, sems.at[0]),
        pltpu.make_async_copy(gain_hbm, gain, sems.at[1]),
    ]
    for copy in small:
        copy.start()
    copies = []
    for step in range(POOL_STEPS):
        part = pl.ds(step * block, block)
        at = 2 + 3 * step
        group = [
            pltpu.make_async_copy(enc_hbm.at[:, part], enc.at[:, part], sems.at[at]),
            pltpu.make_async_copy(wk_hbm.at[part], wkv.at[part, pl.ds(0, HD)], sems.at[at + 1]),
            pltpu.make_async_copy(wv_hbm.at[part], wkv.at[part, pl.ds(HD, HD)], sems.at[at + 2]),
        ]
        copies.append(group)
        if step < DEPTH:
            for copy in group:
                copy.start()
    for copy in small:
        copy.wait()
    before = iota((CAP, CAP), 1) < iota((CAP, CAP), 0)
    start = jnp.sum(jnp.where(before, lengths[...], 0).astype(F32), axis=1, keepdims=True)
    hot = jnp.where(iota((CAP, byte_rows), 1).astype(F32) == start, 1.0, 0.0).astype(BF)
    total = jnp.zeros((CAP, 2 * HD), F32)
    squares = jnp.zeros((CAP, HD), F32)
    held = None
    for step in range(POOL_STEPS + 1):
        if step < POOL_STEPS:
            for copy in copies[step]:
                copy.wait()
            if step + DEPTH < POOL_STEPS:
                for copy in copies[step + DEPTH]:
                    copy.start()
        if held is not None:
            last = slice((step - 1) * block, step * block)
            total += jnp.dot(held, wkv[last, :], preferred_element_type=F32)
        if step < POOL_STEPS:
            part = slice(step * block, (step + 1) * block)
            pooled = jnp.dot(hot, enc[:, part], preferred_element_type=F32)
            for k in range(block // HD):
                piece = pooled[:, k * HD : (k + 1) * HD]
                squares += piece * piece
            held = (pooled * gain[:, part]).astype(BF)
            x_ref[:, part] = held
    scale = lax.rsqrt(jnp.sum(squares, axis=1, keepdims=True) / width + 1e-5)
    scale_ref[...] = jnp.broadcast_to(scale, scale_ref.shape)
    kv_ref[:CAP, :] = (total * scale).astype(BF)
    count = jnp.sum((lengths[...] > 0).astype(F32), axis=1, keepdims=True)
    kv_ref[CAP:, :] = jnp.broadcast_to(count, (TILE, 2 * HD)).astype(BF)


def pool(lengths, enc, gain, wk, wv):
    byte_rows, width = enc.shape
    return pl.pallas_call(
        pool_kernel,
        in_specs=[anywhere()] * 5,
        out_specs=[vmem()] * 3,
        out_shape=[
            jax.ShapeDtypeStruct((ROWS, 2 * HD), BF),
            jax.ShapeDtypeStruct((CAP, width), BF),
            jax.ShapeDtypeStruct((CAP, HD), F32),
        ],
        scratch_shapes=[
            pltpu.VMEM(lengths.shape, jnp.int32),
            pltpu.VMEM(gain.shape, F32),
            pltpu.VMEM((byte_rows, width), BF),
            pltpu.VMEM((width, 2 * HD), BF),
            pltpu.SemaphoreType.DMA((3 * POOL_STEPS + 2,)),
        ],
        compiler_params=params(FULL),
        cost_estimate=pl.CostEstimate(
            flops=2 * CAP * width * (byte_rows + 2 * HD),
            bytes_accessed=2 * width * (byte_rows + CAP + 2 * HD),
            transcendentals=0,
        ),
        name="pool",
    )(lengths, gain, enc, wk, wv)


def query_kernel(x_ref, scale_ref, wq_hbm, q_ref, wq, sems):
    width = wq.shape[0]
    block = width // POOL_STEPS
    copies = []
    for step in range(POOL_STEPS):
        part = pl.ds(step * block, block)
        copies.append(pltpu.make_async_copy(wq_hbm.at[part], wq.at[part], sems.at[step]))
        copies[-1].start()
    total = jnp.zeros(q_ref.shape, F32)
    for step in range(POOL_STEPS):
        copies[step].wait()
        part = slice(step * block, (step + 1) * block)
        total += jnp.dot(x_ref[:, part], wq[part, :], preferred_element_type=F32)
    q_ref[...] = (total * (scale_ref[:, :1] * (LOG2E * HD**-0.5))).astype(BF)


def query(x, wq, scale):
    width, out = wq.shape
    return pl.pallas_call(
        query_kernel,
        in_specs=[vmem(), vmem(), anywhere()],
        out_specs=vmem(),
        out_shape=jax.ShapeDtypeStruct((CAP, out), BF),
        scratch_shapes=[
            pltpu.VMEM((width, out), BF),
            pltpu.SemaphoreType.DMA((POOL_STEPS,)),
        ],
        compiler_params=params(QUERY_LIMIT),
        cost_estimate=pl.CostEstimate(
            flops=2 * CAP * width * out, bytes_accessed=2 * width * (out + CAP), transcendentals=0
        ),
        name="query",
    )(x, scale, wq)


def compact_kernel(index_ref, *refs):
    blocks, out_ref = refs[:8], refs[8]
    x, core = index_ref[1], index_ref[2]
    shifts = (0, 1, 3, 2)
    order = [
        ((x + NX - shift) % NX) * 2 + (core if side == 0 else 1 - core)
        for side in range(2)
        for shift in shifts
    ]
    counts = [ref[CAP : CAP + TILE, :].astype(F32)[:1, :] for ref in blocks]
    lane = iota((1, CAP), 1).astype(F32)
    targets = []
    for i in range(8):
        first = jnp.zeros((1, 2 * HD), F32)
        for k in range(8):
            if k != i:
                first += jnp.where(order[k] < order[i], counts[k], 0.0)
        targets.append(jnp.where(lane < counts[i][:, :CAP], first[:, :CAP] + lane, -1.0))
    sub = iota((TILE, 2 * HD), 0)
    table = jnp.zeros((TILE, 2 * HD), F32)
    for i in range(8):
        table += jnp.where(sub == order[i], counts[i], 0.0)
    out_ref[HALF:UPPER, :] = table.astype(BF)
    for half in range(2):
        row = (iota((HALF, CAP), 0) + half * HALF).astype(F32)
        total = jnp.zeros((HALF, 2 * HD), F32)
        for i in range(8):
            hot = jnp.where(row == targets[i], 1.0, 0.0).astype(BF)
            total += jnp.dot(hot, blocks[i][:CAP, :], preferred_element_type=F32)
        out_ref[half * UPPER : half * UPPER + HALF, :] = total.astype(BF)


def compact(index, blocks):
    return pl.pallas_call(
        compact_kernel,
        in_specs=[pl.BlockSpec(memory_space=pltpu.SMEM)] + [vmem()] * 8,
        out_specs=vmem(),
        out_shape=jax.ShapeDtypeStruct((PIECE, 2 * HD), BF),
        compiler_params=params(),
        name="compact",
    )(index, *blocks)


def single(value):
    return jnp.max(jnp.sum(value, axis=0, keepdims=True)).astype(jnp.int32)


def table_of(ref):
    return ref[HALF:UPPER, :HD].astype(F32)


def heads_of(q_ref, slots):
    q = jnp.concatenate([q_ref[slots, h * HD : (h + 1) * HD] for h in range(4)], axis=0)
    ones = jnp.where(iota((4 * QT, HD), 1) == 0, 1.0, 0.0).astype(BF)
    return jnp.concatenate([q, ones], axis=1)


def place(keys, values, ref, low, to_row, first, live):
    to = pl.ds(pl.multiple_of(first + to_row, TILE), HALF)
    keys[to, :HD] = ref[low : low + HALF, :HD]
    values[to, :] = ref[low : low + HALF, HD:]
    dead = jnp.where(iota((HALF, HD), 0) + to_row < live, 0.0, NEG)
    keys[to, HD:] = dead.astype(BF)


def fill(keys, values, start, rows, bias):
    end = pl.ds(pl.multiple_of(start, TILE), rows)
    keys[end, :HD] = jnp.zeros((rows, HD), BF)
    keys[end, HD:] = jnp.full((rows, HD), bias, BF)
    values[end, :] = jnp.zeros((rows, HD), BF)


def softmax_chunks(q, query_pos, free, chunks, keys, values, scores, top, lsum, acc):
    def score(c):
        rows = pl.ds(pl.multiple_of(c * KEYS, KEYS), KEYS)
        return lax.dot_general(
            q, keys[rows, :], (((1,), (1,)), ((), ())), preferred_element_type=F32
        )

    def keep(c, s):
        scores[c] = s
        best = top[...]
        for k in range(KEYS // HD):
            best = jnp.maximum(best, s[:, k * HD : (k + 1) * HD])
        top[...] = best

    def open_chunk(c, _):
        keep(c, score(c))
        return 0

    def masked_chunk(c, _):
        allowed = c * KEYS + iota((4 * QT, KEYS), 1) <= query_pos
        keep(c, jnp.where(allowed, score(c), NEG))
        return 0

    lax.fori_loop(0, free, open_chunk, 0)
    if query_pos is not None:
        lax.fori_loop(free, chunks, masked_chunk, 0)
    top[...] = jnp.broadcast_to(jnp.max(top[...], axis=1, keepdims=True), top.shape)

    def weigh(c, _):
        best = top[...]
        parts = [jnp.exp2(scores[c, :, k * HD : (k + 1) * HD] - best) for k in range(KEYS // HD)]
        total = parts[0]
        for part in parts[1:]:
            total = total + part
        lsum[...] += total
        p = jnp.concatenate([part.astype(BF) for part in parts], axis=1)
        rows = pl.ds(pl.multiple_of(c * KEYS, KEYS), KEYS)
        acc[...] += jnp.dot(p, values[rows, :], preferred_element_type=F32)
        return 0

    return weigh


def attend_near_kernel(index_ref, q_ref, *refs):
    pieces, (top, lsum, acc, info_ref) = refs[:5], refs[5:9]
    keys, values, scores = refs[9:]
    z, x, core = index_ref[0], index_ref[1], index_ref[2]
    own = x * 2 + core

    own_piece, came, swapped = pieces[0], pieces[1:3], pieces[3:5]
    upward, downward = (came, swapped), (swapped, came)
    planes = [(8 - s, [downward[c][s - 1] for c in range(2)]) for s in (1, 2)]
    planes += [(s, [upward[c][s - 1] for c in range(2)]) for s in (2, 1)]
    planes.append((0, [own_piece, own_piece]))

    lives, most = [], jnp.int32(0)
    for back, (a, b) in planes:
        table = jnp.where(core == 0, table_of(a), table_of(b)) if back else table_of(a)
        lives.append(single(table))
        most = jnp.maximum(most, lives[-1])
    row = iota((TILE, HD), 0)
    own_table = table_of(own_piece)
    before = single(jnp.where(row < own, own_table, 0.0))
    count = single(jnp.where(row == own, own_table, 0.0))
    info_ref[0] = most
    info_ref[1] = count

    first = jnp.int32(0)
    for (back, where), live in zip(planes, lives):
        here = jnp.minimum(live, 2 * HALF)
        for c in range(2 if back else 1):
            wanted = (z >= back) & (core == c) if back else z >= 0

            @pl.when(wanted)
            def _(ref=where[c], here=here, first=first):
                place(keys, values, ref, 0, 0, first, here)
                place(keys, values, ref, UPPER, HALF, first, here)

        if back:
            first = first + jnp.where(z >= back, (here + TILE - 1) // TILE * TILE, 0)
    fill(keys, values, first + 2 * HALF, KEYS, 0.0)
    free = first // KEYS
    chunks = (first + jnp.minimum(before + count, 2 * HALF) + KEYS - 1) // KEYS

    def per_tile(tile, _):
        slots = pl.ds(pl.multiple_of(tile * QT, QT), QT)
        mine = [ref.at[tile] for ref in (top, lsum, acc)]
        mine[0][...] = jnp.full((4 * QT, HD), NEG, F32)
        mine[1][...] = jnp.zeros((4 * QT, HD), F32)
        mine[2][...] = jnp.zeros((4 * QT, HD), F32)
        query_pos = first + before + tile * QT + iota((4 * QT, 1), 0) % QT
        weigh = softmax_chunks(
            heads_of(q_ref, slots), query_pos, free, chunks, keys, values, scores, *mine
        )
        lax.fori_loop(0, chunks, weigh, 0)
        return 0

    lax.fori_loop(0, (count + QT - 1) // QT, per_tile, 0)


def attend_near(index, q, pieces):
    most = 5 * 2 * HALF + KEYS
    most = (most + KEYS - 1) // KEYS * KEYS
    return pl.pallas_call(
        attend_near_kernel,
        in_specs=[pl.BlockSpec(memory_space=pltpu.SMEM)] + [vmem()] * (1 + len(pieces)),
        out_specs=[vmem()] * 3 + [pl.BlockSpec(memory_space=pltpu.SMEM)],
        out_shape=[jax.ShapeDtypeStruct((CAP // QT, 4 * QT, HD), F32)] * 3
        + [jax.ShapeDtypeStruct((2,), jnp.int32)],
        scratch_shapes=[
            pltpu.VMEM((most, 2 * HD), BF),
            pltpu.VMEM((most, HD), BF),
            pltpu.VMEM((most // KEYS, 4 * QT, KEYS), F32),
        ],
        compiler_params=params(),
        cost_estimate=pl.CostEstimate(
            flops=12 * QT * most * 3 * HD * 2, bytes_accessed=1 << 23, transcendentals=8 * QT * most
        ),
        name="attend_near",
    )(index, q, *pieces)


def add_tile(tile, q_ref, given, mine, chunks, keys, values, scores):
    slots = pl.ds(pl.multiple_of(tile * QT, QT), QT)
    mine[0][...] = given[0][tile]
    weigh = softmax_chunks(
        heads_of(q_ref, slots), None, chunks, chunks, keys, values, scores, *mine
    )
    factor = jnp.exp2(given[0][tile] - mine[0][...])
    mine[1][...] = given[1][tile] * factor
    mine[2][...] = given[2][tile] * factor
    lax.fori_loop(0, chunks, weigh, 0)


def attend_more_kernel(index_ref, info_ref, q_ref, came, swapped, top, lsum, acc, *refs):
    results, out_info, (keys, values, scores) = refs[:3], refs[3], refs[4:]
    z, core = index_ref[0], index_ref[2]
    first, most = jnp.int32(0), info_ref[0]
    for back, where in ((5, (swapped, came)), (3, (came, swapped))):
        live = single(jnp.where(core == 0, table_of(where[0]), table_of(where[1])))
        most = jnp.maximum(most, live)
        here = jnp.minimum(live, 2 * HALF)
        for c in range(2):

            @pl.when((z >= back) & (core == c))
            def _(ref=where[c], here=here, first=first):
                place(keys, values, ref, 0, 0, first, here)
                place(keys, values, ref, UPPER, HALF, first, here)

        first = first + jnp.where(z >= back, (here + TILE - 1) // TILE * TILE, 0)
    fill(keys, values, first, KEYS, NEG)
    chunks = (first + KEYS - 1) // KEYS
    out_info[0] = most
    out_info[1] = info_ref[1]

    def per_tile(tile, _):
        mine = [ref.at[tile] for ref in results]
        add_tile(tile, q_ref, (top, lsum, acc), mine, chunks, keys, values, scores)
        return 0

    lax.fori_loop(0, (info_ref[1] + QT - 1) // QT, per_tile, 0)


def attend_more(index, q, came, swapped, state, info):
    most = 2 * 2 * HALF + KEYS
    most = (most + KEYS - 1) // KEYS * KEYS
    return pl.pallas_call(
        attend_more_kernel,
        in_specs=[pl.BlockSpec(memory_space=pltpu.SMEM)] * 2 + [vmem()] * 6,
        out_specs=[vmem()] * 3 + [pl.BlockSpec(memory_space=pltpu.SMEM)],
        out_shape=[jax.ShapeDtypeStruct(value.shape, F32) for value in state]
        + [jax.ShapeDtypeStruct((2,), jnp.int32)],
        scratch_shapes=[
            pltpu.VMEM((most, 2 * HD), BF),
            pltpu.VMEM((most, HD), BF),
            pltpu.VMEM((most // KEYS, 4 * QT, KEYS), F32),
        ],
        compiler_params=params(),
        cost_estimate=pl.CostEstimate(
            flops=12 * QT * most * 3 * HD * 2, bytes_accessed=1 << 23, transcendentals=8 * QT * most
        ),
        name="attend_more",
    )(index, info, q, came, swapped, *state)


def attend_far_kernel(index_ref, info_ref, q_ref, wout_ref, came, swapped, top, lsum, acc, *refs):
    outs, flag_ref = refs[:4], refs[4]
    keys, values, scores, peak, total, sums = refs[5:]
    z, core, y = index_ref[0], index_ref[2], index_ref[3]
    for out in outs:
        out[...] = jnp.zeros_like(out)
    live = single(table_of_far(came, core))
    flag_ref[0] = (jnp.maximum(info_ref[0], live) > 2 * HALF).astype(jnp.int32)
    count = info_ref[1]
    here = jnp.minimum(live, 2 * HALF)
    for c, lower, upper in ((0, came, swapped), (1, swapped, came)):

        @pl.when(core == c)
        def _(lower=lower, upper=upper):
            place(keys, values, lower, 0, 0, 0, here)
            place(keys, values, upper, TILE, HALF, 0, here)

    fill(keys, values, 2 * HALF, 2 * KEYS - 2 * HALF, NEG)
    chunks = jnp.where(z >= 4, (here + KEYS - 1) // KEYS, 0)

    def per_tile(tile, _):
        slots = pl.ds(pl.multiple_of(tile * QT, QT), QT)
        add_tile(
            tile, q_ref, (top, lsum, acc), (peak, total, sums), chunks, keys, values, scores
        )
        a = (sums[...] / jnp.sum(total[...], axis=1, keepdims=True)).astype(BF)
        a = jnp.concatenate([a[h * QT : (h + 1) * QT, :] for h in range(4)], axis=1)
        for k in range(4):
            cols = pl.ds(pl.multiple_of(((y + k) % 4) * 256, 256), 256)
            outs[k][slots, :] = jnp.dot(
                a, wout_ref[:, cols], preferred_element_type=F32
            ).astype(BF)
        return 0

    lax.fori_loop(0, (count + QT - 1) // QT, per_tile, 0)


def table_of_far(came, core):
    low, high = came[:TILE, :HD].astype(F32), came[HALF:UPPER, :HD].astype(F32)
    return jnp.where(core == 0, high, low)


def attend_far(index, info, q, wout, came, swapped, state):
    *parts, flag = pl.pallas_call(
        attend_far_kernel,
        in_specs=[pl.BlockSpec(memory_space=pltpu.SMEM)] * 2 + [vmem()] * 7,
        out_specs=[vmem()] * 4 + [pl.BlockSpec(memory_space=pltpu.SMEM)],
        out_shape=[jax.ShapeDtypeStruct((CAP, 256), BF)] * 4
        + [jax.ShapeDtypeStruct((1,), jnp.int32)],
        scratch_shapes=[
            pltpu.VMEM((2 * KEYS, 2 * HD), BF),
            pltpu.VMEM((2 * KEYS, HD), BF),
            pltpu.VMEM((2, 4 * QT, KEYS), F32),
        ]
        + [pltpu.VMEM((4 * QT, HD), F32)] * 3,
        compiler_params=params(),
        name="attend_far",
    )(index, info, q, wout, came, swapped, *state)
    return parts, flag[0]


def attend_any(kv, q, lengths, wout, y):
    device = lax.axis_index("seq")
    devices = lax.axis_size("seq")
    queries = q.reshape(CAP, 4, HD)
    slot = jnp.arange(CAP, dtype=jnp.int32)

    def step(turn, carry):
        block, top, total, weighted = carry
        source = (device - turn) % devices
        keys, values = block[:CAP, :HD], block[:CAP, HD:]
        live = block[CAP, 0].astype(jnp.int32)
        s = jnp.einsum("wgd,rd->wgr", queries, keys, preferred_element_type=F32)
        later = (source == device) & (slot[None, :] > slot[:, None])
        allowed = ((slot < live)[None, :] & (source <= device) & ~later)[:, None, :]
        s = jnp.where(allowed, s, NEG)
        new = jnp.maximum(top, jnp.max(s, axis=2))
        factor = jnp.exp2(top - new)
        w = jnp.where(allowed, jnp.exp2(s - new[..., None]), 0.0)
        total = total * factor + jnp.sum(w, axis=2)
        weighted = weighted * factor[..., None] + jnp.einsum(
            "wgr,rd->wgd", w.astype(BF), values, preferred_element_type=F32
        )
        block = lax.ppermute(block, "seq", [(i, (i + 1) % devices) for i in range(devices)])
        return block, new, total, weighted

    start = (
        kv,
        jnp.full((CAP, 4), NEG, F32),
        jnp.zeros((CAP, 4), F32),
        jnp.zeros((CAP, 4, HD), F32),
    )
    _, _, total, weighted = lax.fori_loop(0, devices, step, start)
    a = (weighted / total[..., None]).reshape(CAP, 4 * HD).astype(BF)
    part = jnp.dot(a, wout, preferred_element_type=F32).astype(BF)
    return [lax.dynamic_slice_in_dim(part, ((y + k) % 4) * 256, 256, 1) for k in range(4)]


def mix_kernel(len_ref, skip_ref, p0, p1, p2, p3, mixed_ref, tail_ref):
    byte_rows = skip_ref.shape[0]
    lengths = len_ref[...].astype(F32)
    inner = p0[...].astype(F32) + p1[...].astype(F32) + p2[...].astype(F32) + p3[...].astype(F32)
    i, j = iota((CAP, CAP), 0), iota((CAP, CAP), 1)
    column = jnp.sum(jnp.where(i == j, lengths, 0.0), axis=1, keepdims=True)
    start = jnp.sum(jnp.where(i < j, column, 0.0), axis=0, keepdims=True)
    at = iota((byte_rows, CAP), 0).astype(F32)
    hot = jnp.where((at >= start) & (at < start + lengths), 1.0, 0.0).astype(BF)
    up = jnp.dot(hot, inner.astype(BF), preferred_element_type=F32)
    mixed = (skip_ref[...].astype(F32) + up).astype(BF)
    mixed_ref[...] = mixed
    tail_ref[...] = mixed[byte_rows - HALO :, :]


def mix(lengths, skip, parts):
    return pl.pallas_call(
        mix_kernel,
        in_specs=[vmem()] * 6,
        out_specs=[vmem()] * 2,
        out_shape=[
            jax.ShapeDtypeStruct(skip.shape, BF),
            jax.ShapeDtypeStruct((HALO, skip.shape[1]), BF),
        ],
        compiler_params=params(),
        name="mix",
    )(lengths, skip, *parts)


def filtered(window, taps):
    rows = window.shape[0] - HALO
    total = jnp.zeros((rows, window.shape[1]), F32)
    lags = taps.shape[0]
    for r in range(8):
        moved = window[8 - r : rows + HALO - r, :]
        for lag in range(r, lags, 8):
            low = HALO - 8 - (lag - r)
            total += taps[lag : lag + 1, :] * moved[low : low + rows, :]
    return (window[HALO:, :] + total / (1.0 + jnp.exp(-total))).astype(BF)


def conv_kernel(mixed_ref, taps_ref, out_ref, ext):
    byte_rows, channels = mixed_ref.shape
    ext[:HALO, :] = jnp.zeros((HALO, channels), F32)
    ext[HALO:, :] = mixed_ref[...].astype(F32)
    block = 128
    lags = taps_ref.shape[0]

    for first in range(0, byte_rows, block):
        for low in range(0, channels, 128):
            part = slice(low, low + 128)
            total = jnp.zeros((block, 128), F32)
            for lag in range(lags):
                start = first + HALO - lag
                total += taps_ref[lag : lag + 1, part] * ext[start : start + block, part]
            here = ext[first + HALO : first + HALO + block, part]
            silu = total / (1.0 + jnp.exp(-total))
            out_ref[first : first + block, part] = (here + silu).astype(BF)


def rim_kernel(given_hbm, rim_ref, mixed_ref, taps_ref, out_hbm, rows, sem):
    del given_hbm
    for low in range(0, mixed_ref.shape[1], 128):
        part = slice(low, low + 128)
        window = jnp.concatenate([rim_ref[:, part], mixed_ref[:HALO, part]], axis=0).astype(F32)
        rows[:, part] = filtered(window, taps_ref[:, part])
    copy = pltpu.make_async_copy(rows, out_hbm.at[pl.ds(0, HALO)], sem)
    copy.start()
    copy.wait()


def convolve(mixed, taps):
    return pl.pallas_call(
        conv_kernel,
        in_specs=[vmem()] * 2,
        out_specs=vmem(),
        out_shape=jax.ShapeDtypeStruct(mixed.shape, BF),
        scratch_shapes=[pltpu.VMEM((HALO + mixed.shape[0], mixed.shape[1]), F32)],
        compiler_params=params(),
        cost_estimate=pl.CostEstimate(
            flops=2 * mixed.size * taps.shape[0], bytes_accessed=16 * mixed.size, transcendentals=0
        ),
        name="convolve",
    )(mixed, taps)


def first_rows(given, rim, mixed, taps):
    return pl.pallas_call(
        rim_kernel,
        in_specs=[anywhere()] + [vmem()] * 3,
        out_specs=anywhere(),
        out_shape=jax.ShapeDtypeStruct(given.shape, BF),
        input_output_aliases={0: 0},
        scratch_shapes=[pltpu.VMEM((HALO, mixed.shape[1]), BF), pltpu.SemaphoreType.DMA],
        compiler_params=params(),
        name="first_rows",
    )(given, rim, mixed, taps)


def seq_permute(value, move):
    pairs = []
    for z in range(NZ):
        for x in range(NX):
            for core in range(2):
                tz, tx, tc = move(z, x, core)
                target = ((tz % NZ) * NX + tx % NX) * 2 + tc
                pairs.append(((z * NX + x) * 2 + core, target))
    return lax.ppermute(value, "seq", pairs)


def along_x(value, steps):
    return seq_permute(value, lambda z, x, c: (z, x + steps, c))


def round_z(value):
    return seq_permute(value, lambda z, x, c: (z + 1 - 2 * c, x, c))


def swap(value):
    return seq_permute(value, lambda z, x, c: (z, x, 1 - c))


def per_device(enc, span_len, skip, gain, wq, wk, wv, wout, taps):
    seq = lax.axis_index("seq")
    y = lax.axis_index("section")
    index = jnp.stack([seq // (2 * NX), (seq // 2) % NX, seq % 2, y]).astype(jnp.int32)
    kv, x, scale = pool(span_len, enc, gain.reshape(1, -1), wk, wv)
    across = along_x(kv, 2)
    column = [kv, along_x(kv, 1), along_x(kv, -1), across]
    plane = compact(index, column + [swap(v) for v in column])
    first, q = lax.optimization_barrier((round_z(plane), query(x, wq, scale)))
    came = [first]
    came.append(round_z(first))
    near = attend_near(index, q, [plane] + came + [swap(piece) for piece in came])
    third, (*state, info) = lax.optimization_barrier((round_z(came[-1]), near))
    far = round_z(lax.dynamic_slice_in_dim(third, (seq % 2) * HALF, UPPER, 0))
    more = attend_more(index, q, third, swap(third), state, info)
    far, (*state, info) = lax.optimization_barrier((far, more))
    parts, crowded = attend_far(index, info, q, wout, far, swap(far), state)
    parts = lax.cond(
        crowded > 0, lambda _: attend_any(kv, q, span_len, wout, y), lambda given: given, parts
    )
    sent = [
        lax.ppermute(parts[k], "section", [(i, (i + k) % 4) for i in range(4)]) for k in (2, 1, 3)
    ]
    mixed, tail = mix(span_len, skip, [parts[0]] + sent)
    rim = lax.ppermute(tail, "seq", [(i, i + 1) for i in range(2 * NX * NZ - 1)])
    return first_rows(convolve(mixed, taps), rim, mixed, taps)


def solution(mesh):
    return jax.shard_map(
        per_device,
        mesh=mesh,
        in_specs=(
            P("seq", None),
            P("seq", None),
            P("seq", "section"),
            P(),
            P(None, "section"),
            P(None, "section"),
            P(None, "section"),
            P("section", None),
            P(None, "section"),
        ),
        out_specs=P("seq", "section"),
        check_vma=False,
    )
```

```python
import math

import jax
import jax.numpy as jnp
from jax import lax
from jax.experimental import pallas as pl
from jax.experimental.pallas import tpu as pltpu
from jax.sharding import PartitionSpec as P

HD = 128
CAP = 192
TILE = 16
ROWS = CAP + TILE
NX = 4
NZ = 8
HALF = 352
UPPER = HALF + TILE
PIECE = UPPER + HALF
QT = 96
KEYS = 512
POOL_STEPS = 4
DEPTH = 4
FULL = 62
QUERY_LIMIT = 60
HALO = 32
LOG2E = math.log2(math.e)
NEG = -1e30
MIB = 1 << 20
BF = jnp.bfloat16
F32 = jnp.float32


def vmem():
    return pl.BlockSpec(memory_space=pltpu.VMEM)


def anywhere():
    return pl.BlockSpec(memory_space=pl.ANY)


def params(limit=48):
    return pltpu.CompilerParams(vmem_limit_bytes=limit * MIB)


def iota(shape, dim):
    return lax.broadcasted_iota(jnp.int32, shape, dim)


def pool_kernel(len_hbm, gain_hbm, enc_hbm, wk_hbm, wv_hbm, kv_ref, x_ref, scale_ref, lengths, gain, enc, wkv, sems):
    byte_rows, width = enc.shape
    block = width // POOL_STEPS
    small = [
        pltpu.make_async_copy(len_hbm, lengths, sems.at[0]),
        pltpu.make_async_copy(gain_hbm, gain, sems.at[1]),
    ]
    for copy in small:
        copy.start()
    copies = []
    for step in range(POOL_STEPS):
        part = pl.ds(step * block, block)
        at = 2 + 3 * step
        group = [
            pltpu.make_async_copy(enc_hbm.at[:, part], enc.at[:, part], sems.at[at]),
            pltpu.make_async_copy(wk_hbm.at[part], wkv.at[part, pl.ds(0, HD)], sems.at[at + 1]),
            pltpu.make_async_copy(wv_hbm.at[part], wkv.at[part, pl.ds(HD, HD)], sems.at[at + 2]),
        ]
        copies.append(group)
        if step < DEPTH:
            for copy in group:
                copy.start()
    for copy in small:
        copy.wait()
    before = iota((CAP, CAP), 1) < iota((CAP, CAP), 0)
    start = jnp.sum(jnp.where(before, lengths[...], 0).astype(F32), axis=1, keepdims=True)
    hot = jnp.where(iota((CAP, byte_rows), 1).astype(F32) == start, 1.0, 0.0).astype(BF)
    total = jnp.zeros((CAP, 2 * HD), F32)
    squares = jnp.zeros((CAP, HD), F32)
    held = None
    for step in range(POOL_STEPS + 1):
        if step < POOL_STEPS:
            for copy in copies[step]:
                copy.wait()
            if step + DEPTH < POOL_STEPS:
                for copy in copies[step + DEPTH]:
                    copy.start()
        if held is not None:
            last = slice((step - 1) * block, step * block)
            total += jnp.dot(held, wkv[last, :], preferred_element_type=F32)
        if step < POOL_STEPS:
            part = slice(step * block, (step + 1) * block)
            pooled = jnp.dot(hot, enc[:, part], preferred_element_type=F32)
            for k in range(block // HD):
                piece = pooled[:, k * HD : (k + 1) * HD]
                squares += piece * piece
            held = (pooled * gain[:, part]).astype(BF)
            x_ref[:, part] = held
    scale = lax.rsqrt(jnp.sum(squares, axis=1, keepdims=True) / width + 1e-5)
    scale_ref[...] = jnp.broadcast_to(scale, scale_ref.shape)
    kv_ref[:CAP, :] = (total * scale).astype(BF)
    count = jnp.sum((lengths[...] > 0).astype(F32), axis=1, keepdims=True)
    kv_ref[CAP:, :] = jnp.broadcast_to(count, (TILE, 2 * HD)).astype(BF)


def pool(lengths, enc, gain, wk, wv):
    byte_rows, width = enc.shape
    return pl.pallas_call(
        pool_kernel,
        in_specs=[anywhere()] * 5,
        out_specs=[vmem()] * 3,
        out_shape=[
            jax.ShapeDtypeStruct((ROWS, 2 * HD), BF),
            jax.ShapeDtypeStruct((CAP, width), BF),
            jax.ShapeDtypeStruct((CAP, HD), F32),
        ],
        scratch_shapes=[
            pltpu.VMEM(lengths.shape, jnp.int32),
            pltpu.VMEM(gain.shape, F32),
            pltpu.VMEM((byte_rows, width), BF),
            pltpu.VMEM((width, 2 * HD), BF),
            pltpu.SemaphoreType.DMA((3 * POOL_STEPS + 2,)),
        ],
        compiler_params=params(FULL),
        cost_estimate=pl.CostEstimate(
            flops=2 * CAP * width * (byte_rows + 2 * HD),
            bytes_accessed=2 * width * (byte_rows + CAP + 2 * HD),
            transcendentals=0,
        ),
        name="pool",
    )(lengths, gain, enc, wk, wv)


def query_kernel(x_ref, scale_ref, wq_hbm, q_ref, wq, sems):
    width = wq.shape[0]
    block = width // POOL_STEPS
    copies = []
    for step in range(POOL_STEPS):
        part = pl.ds(step * block, block)
        copies.append(pltpu.make_async_copy(wq_hbm.at[part], wq.at[part], sems.at[step]))
        copies[-1].start()
    total = jnp.zeros(q_ref.shape, F32)
    for step in range(POOL_STEPS):
        copies[step].wait()
        part = slice(step * block, (step + 1) * block)
        total += jnp.dot(x_ref[:, part], wq[part, :], preferred_element_type=F32)
    q_ref[...] = (total * (scale_ref[:, :1] * (LOG2E * HD**-0.5))).astype(BF)


def query(x, wq, scale):
    width, out = wq.shape
    return pl.pallas_call(
        query_kernel,
        in_specs=[vmem(), vmem(), anywhere()],
        out_specs=vmem(),
        out_shape=jax.ShapeDtypeStruct((CAP, out), BF),
        scratch_shapes=[
            pltpu.VMEM((width, out), BF),
            pltpu.SemaphoreType.DMA((POOL_STEPS,)),
        ],
        compiler_params=params(QUERY_LIMIT),
        cost_estimate=pl.CostEstimate(
            flops=2 * CAP * width * out, bytes_accessed=2 * width * (out + CAP), transcendentals=0
        ),
        name="query",
    )(x, scale, wq)


def compact_kernel(index_ref, *refs):
    blocks, out_ref = refs[:8], refs[8]
    x, core = index_ref[1], index_ref[2]
    shifts = (0, 1, 3, 2)
    order = [
        ((x + NX - shift) % NX) * 2 + (core if side == 0 else 1 - core)
        for side in range(2)
        for shift in shifts
    ]
    counts = [ref[CAP : CAP + TILE, :].astype(F32)[:1, :] for ref in blocks]
    lane = iota((1, CAP), 1).astype(F32)
    targets = []
    for i in range(8):
        first = jnp.zeros((1, 2 * HD), F32)
        for k in range(8):
            if k != i:
                first += jnp.where(order[k] < order[i], counts[k], 0.0)
        targets.append(jnp.where(lane < counts[i][:, :CAP], first[:, :CAP] + lane, -1.0))
    sub = iota((TILE, 2 * HD), 0)
    table = jnp.zeros((TILE, 2 * HD), F32)
    for i in range(8):
        table += jnp.where(sub == order[i], counts[i], 0.0)
    out_ref[HALF:UPPER, :] = table.astype(BF)
    target = jnp.concatenate(targets, axis=1)
    rows = jnp.concatenate([ref[:CAP, :] for ref in blocks], axis=0)
    for half in range(2):
        row = (iota((HALF, 8 * CAP), 0) + half * HALF).astype(F32)
        hot = jnp.where(row == target, 1.0, 0.0).astype(BF)
        total = jnp.dot(hot, rows, preferred_element_type=F32)
        out_ref[half * UPPER : half * UPPER + HALF, :] = total.astype(BF)


def compact(index, blocks):
    return pl.pallas_call(
        compact_kernel,
        in_specs=[pl.BlockSpec(memory_space=pltpu.SMEM)] + [vmem()] * 8,
        out_specs=vmem(),
        out_shape=jax.ShapeDtypeStruct((PIECE, 2 * HD), BF),
        compiler_params=params(),
        name="compact",
    )(index, *blocks)


def single(value):
    return jnp.max(jnp.sum(value, axis=0, keepdims=True)).astype(jnp.int32)


def table_of(ref):
    return ref[HALF:UPPER, :HD].astype(F32)


def heads_of(q_ref, slots):
    q = jnp.concatenate([q_ref[slots, h * HD : (h + 1) * HD] for h in range(4)], axis=0)
    ones = jnp.where(iota((4 * QT, HD), 1) == 0, 1.0, 0.0).astype(BF)
    return jnp.concatenate([q, ones], axis=1)


def place(keys, values, ref, low, to_row, first, live):
    to = pl.ds(pl.multiple_of(first + to_row, TILE), HALF)
    keys[to, :HD] = ref[low : low + HALF, :HD]
    values[to, :] = ref[low : low + HALF, HD:]
    dead = jnp.where(iota((HALF, HD), 0) + to_row < live, 0.0, NEG)
    keys[to, HD:] = dead.astype(BF)


def fill(keys, values, start, rows, bias):
    end = pl.ds(pl.multiple_of(start, TILE), rows)
    keys[end, :HD] = jnp.zeros((rows, HD), BF)
    keys[end, HD:] = jnp.full((rows, HD), bias, BF)
    values[end, :] = jnp.zeros((rows, HD), BF)


def softmax_chunks(q, query_pos, free, chunks, keys, values, scores, top, lsum, acc):
    def score(c):
        rows = pl.ds(pl.multiple_of(c * KEYS, KEYS), KEYS)
        return lax.dot_general(
            q, keys[rows, :], (((1,), (1,)), ((), ())), preferred_element_type=F32
        )

    def keep(c, s):
        scores[c] = s
        best = top[...]
        for k in range(KEYS // HD):
            best = jnp.maximum(best, s[:, k * HD : (k + 1) * HD])
        top[...] = best

    def open_chunk(c, _):
        keep(c, score(c))
        return 0

    def masked_chunk(c, _):
        allowed = c * KEYS + iota((4 * QT, KEYS), 1) <= query_pos
        keep(c, jnp.where(allowed, score(c), NEG))
        return 0

    lax.fori_loop(0, free, open_chunk, 0)
    if query_pos is not None:
        lax.fori_loop(free, chunks, masked_chunk, 0)
    top[...] = jnp.broadcast_to(jnp.max(top[...], axis=1, keepdims=True), top.shape)

    def weigh(c, _):
        best = top[...]
        parts = [jnp.exp2(scores[c, :, k * HD : (k + 1) * HD] - best) for k in range(KEYS // HD)]
        total = parts[0]
        for part in parts[1:]:
            total = total + part
        lsum[...] += total
        p = jnp.concatenate([part.astype(BF) for part in parts], axis=1)
        rows = pl.ds(pl.multiple_of(c * KEYS, KEYS), KEYS)
        acc[...] += jnp.dot(p, values[rows, :], preferred_element_type=F32)
        return 0

    return weigh


def attend_near_kernel(index_ref, q_ref, *refs):
    pieces, (top, lsum, acc, info_ref) = refs[:5], refs[5:9]
    keys, values, scores = refs[9:]
    z, x, core = index_ref[0], index_ref[1], index_ref[2]
    own = x * 2 + core

    own_piece, came, swapped = pieces[0], pieces[1:3], pieces[3:5]
    upward, downward = (came, swapped), (swapped, came)
    planes = [(8 - s, [downward[c][s - 1] for c in range(2)]) for s in (1, 2)]
    planes += [(s, [upward[c][s - 1] for c in range(2)]) for s in (2, 1)]
    planes.append((0, [own_piece, own_piece]))

    lives, most = [], jnp.int32(0)
    for back, (a, b) in planes:
        table = jnp.where(core == 0, table_of(a), table_of(b)) if back else table_of(a)
        lives.append(single(table))
        most = jnp.maximum(most, lives[-1])
    row = iota((TILE, HD), 0)
    own_table = table_of(own_piece)
    before = single(jnp.where(row < own, own_table, 0.0))
    count = single(jnp.where(row == own, own_table, 0.0))
    info_ref[0] = most
    info_ref[1] = count

    first = jnp.int32(0)
    for (back, where), live in zip(planes, lives):
        here = jnp.minimum(live, 2 * HALF)
        for c in range(2 if back else 1):
            wanted = (z >= back) & (core == c) if back else z >= 0

            @pl.when(wanted)
            def _(ref=where[c], here=here, first=first):
                place(keys, values, ref, 0, 0, first, here)
                place(keys, values, ref, UPPER, HALF, first, here)

        if back:
            first = first + jnp.where(z >= back, (here + TILE - 1) // TILE * TILE, 0)
    fill(keys, values, first + 2 * HALF, KEYS, 0.0)
    free = first // KEYS
    chunks = (first + jnp.minimum(before + count, 2 * HALF) + KEYS - 1) // KEYS

    def per_tile(tile, _):
        slots = pl.ds(pl.multiple_of(tile * QT, QT), QT)
        mine = [ref.at[tile] for ref in (top, lsum, acc)]
        mine[0][...] = jnp.full((4 * QT, HD), NEG, F32)
        mine[1][...] = jnp.zeros((4 * QT, HD), F32)
        mine[2][...] = jnp.zeros((4 * QT, HD), F32)
        query_pos = first + before + tile * QT + iota((4 * QT, 1), 0) % QT
        weigh = softmax_chunks(
            heads_of(q_ref, slots), query_pos, free, chunks, keys, values, scores, *mine
        )
        lax.fori_loop(0, chunks, weigh, 0)
        return 0

    lax.fori_loop(0, (count + QT - 1) // QT, per_tile, 0)


def attend_near(index, q, pieces):
    most = 5 * 2 * HALF + KEYS
    most = (most + KEYS - 1) // KEYS * KEYS
    return pl.pallas_call(
        attend_near_kernel,
        in_specs=[pl.BlockSpec(memory_space=pltpu.SMEM)] + [vmem()] * (1 + len(pieces)),
        out_specs=[vmem()] * 3 + [pl.BlockSpec(memory_space=pltpu.SMEM)],
        out_shape=[jax.ShapeDtypeStruct((CAP // QT, 4 * QT, HD), F32)] * 3
        + [jax.ShapeDtypeStruct((2,), jnp.int32)],
        scratch_shapes=[
            pltpu.VMEM((most, 2 * HD), BF),
            pltpu.VMEM((most, HD), BF),
            pltpu.VMEM((most // KEYS, 4 * QT, KEYS), F32),
        ],
        compiler_params=params(),
        cost_estimate=pl.CostEstimate(
            flops=12 * QT * most * 3 * HD * 2, bytes_accessed=1 << 23, transcendentals=8 * QT * most
        ),
        name="attend_near",
    )(index, q, *pieces)


def add_tile(tile, q_ref, given, mine, chunks, keys, values, scores):
    slots = pl.ds(pl.multiple_of(tile * QT, QT), QT)
    mine[0][...] = given[0][tile]
    weigh = softmax_chunks(
        heads_of(q_ref, slots), None, chunks, chunks, keys, values, scores, *mine
    )
    factor = jnp.exp2(given[0][tile] - mine[0][...])
    mine[1][...] = given[1][tile] * factor
    mine[2][...] = given[2][tile] * factor
    lax.fori_loop(0, chunks, weigh, 0)


def attend_more_kernel(index_ref, info_ref, q_ref, came, swapped, top, lsum, acc, *refs):
    results, out_info, (keys, values, scores) = refs[:3], refs[3], refs[4:]
    z, core = index_ref[0], index_ref[2]
    first, most = jnp.int32(0), info_ref[0]
    for back, where in ((5, (swapped, came)), (3, (came, swapped))):
        live = single(jnp.where(core == 0, table_of(where[0]), table_of(where[1])))
        most = jnp.maximum(most, live)
        here = jnp.minimum(live, 2 * HALF)
        for c in range(2):

            @pl.when((z >= back) & (core == c))
            def _(ref=where[c], here=here, first=first):
                place(keys, values, ref, 0, 0, first, here)
                place(keys, values, ref, UPPER, HALF, first, here)

        first = first + jnp.where(z >= back, (here + TILE - 1) // TILE * TILE, 0)
    fill(keys, values, first, KEYS, NEG)
    chunks = (first + KEYS - 1) // KEYS
    out_info[0] = most
    out_info[1] = info_ref[1]

    def per_tile(tile, _):
        mine = [ref.at[tile] for ref in results]
        add_tile(tile, q_ref, (top, lsum, acc), mine, chunks, keys, values, scores)
        return 0

    lax.fori_loop(0, (info_ref[1] + QT - 1) // QT, per_tile, 0)


def attend_more(index, q, came, swapped, state, info):
    most = 2 * 2 * HALF + KEYS
    most = (most + KEYS - 1) // KEYS * KEYS
    return pl.pallas_call(
        attend_more_kernel,
        in_specs=[pl.BlockSpec(memory_space=pltpu.SMEM)] * 2 + [vmem()] * 6,
        out_specs=[vmem()] * 3 + [pl.BlockSpec(memory_space=pltpu.SMEM)],
        out_shape=[jax.ShapeDtypeStruct(value.shape, F32) for value in state]
        + [jax.ShapeDtypeStruct((2,), jnp.int32)],
        scratch_shapes=[
            pltpu.VMEM((most, 2 * HD), BF),
            pltpu.VMEM((most, HD), BF),
            pltpu.VMEM((most // KEYS, 4 * QT, KEYS), F32),
        ],
        compiler_params=params(),
        cost_estimate=pl.CostEstimate(
            flops=12 * QT * most * 3 * HD * 2, bytes_accessed=1 << 23, transcendentals=8 * QT * most
        ),
        name="attend_more",
    )(index, info, q, came, swapped, *state)


def attend_far_kernel(index_ref, info_ref, q_ref, wout_ref, came, swapped, top, lsum, acc, *refs):
    outs, flag_ref = refs[:4], refs[4]
    keys, values, scores, peak, total, sums = refs[5:]
    z, core, y = index_ref[0], index_ref[2], index_ref[3]
    for out in outs:
        out[...] = jnp.zeros_like(out)
    live = single(table_of_far(came, core))
    flag_ref[0] = (jnp.maximum(info_ref[0], live) > 2 * HALF).astype(jnp.int32)
    count = info_ref[1]
    here = jnp.minimum(live, 2 * HALF)
    for c, lower, upper in ((0, came, swapped), (1, swapped, came)):

        @pl.when(core == c)
        def _(lower=lower, upper=upper):
            place(keys, values, lower, 0, 0, 0, here)
            place(keys, values, upper, TILE, HALF, 0, here)

    fill(keys, values, 2 * HALF, 2 * KEYS - 2 * HALF, NEG)
    chunks = jnp.where(z >= 4, (here + KEYS - 1) // KEYS, 0)

    def per_tile(tile, _):
        slots = pl.ds(pl.multiple_of(tile * QT, QT), QT)
        add_tile(
            tile, q_ref, (top, lsum, acc), (peak, total, sums), chunks, keys, values, scores
        )
        a = (sums[...] / jnp.sum(total[...], axis=1, keepdims=True)).astype(BF)
        a = jnp.concatenate([a[h * QT : (h + 1) * QT, :] for h in range(4)], axis=1)
        for k in range(4):
            cols = pl.ds(pl.multiple_of(((y + k) % 4) * 256, 256), 256)
            outs[k][slots, :] = jnp.dot(
                a, wout_ref[:, cols], preferred_element_type=F32
            ).astype(BF)
        return 0

    lax.fori_loop(0, (count + QT - 1) // QT, per_tile, 0)


def table_of_far(came, core):
    low, high = came[:TILE, :HD].astype(F32), came[HALF:UPPER, :HD].astype(F32)
    return jnp.where(core == 0, high, low)


def attend_far(index, info, q, wout, came, swapped, state):
    *parts, flag = pl.pallas_call(
        attend_far_kernel,
        in_specs=[pl.BlockSpec(memory_space=pltpu.SMEM)] * 2 + [vmem()] * 7,
        out_specs=[vmem()] * 4 + [pl.BlockSpec(memory_space=pltpu.SMEM)],
        out_shape=[jax.ShapeDtypeStruct((CAP, 256), BF)] * 4
        + [jax.ShapeDtypeStruct((1,), jnp.int32)],
        scratch_shapes=[
            pltpu.VMEM((2 * KEYS, 2 * HD), BF),
            pltpu.VMEM((2 * KEYS, HD), BF),
            pltpu.VMEM((2, 4 * QT, KEYS), F32),
        ]
        + [pltpu.VMEM((4 * QT, HD), F32)] * 3,
        compiler_params=params(),
        name="attend_far",
    )(index, info, q, wout, came, swapped, *state)
    return parts, flag[0]


def attend_any(kv, q, lengths, wout, y):
    device = lax.axis_index("seq")
    devices = lax.axis_size("seq")
    queries = q.reshape(CAP, 4, HD)
    slot = jnp.arange(CAP, dtype=jnp.int32)

    def step(turn, carry):
        block, top, total, weighted = carry
        source = (device - turn) % devices
        keys, values = block[:CAP, :HD], block[:CAP, HD:]
        live = block[CAP, 0].astype(jnp.int32)
        s = jnp.einsum("wgd,rd->wgr", queries, keys, preferred_element_type=F32)
        later = (source == device) & (slot[None, :] > slot[:, None])
        allowed = ((slot < live)[None, :] & (source <= device) & ~later)[:, None, :]
        s = jnp.where(allowed, s, NEG)
        new = jnp.maximum(top, jnp.max(s, axis=2))
        factor = jnp.exp2(top - new)
        w = jnp.where(allowed, jnp.exp2(s - new[..., None]), 0.0)
        total = total * factor + jnp.sum(w, axis=2)
        weighted = weighted * factor[..., None] + jnp.einsum(
            "wgr,rd->wgd", w.astype(BF), values, preferred_element_type=F32
        )
        block = lax.ppermute(block, "seq", [(i, (i + 1) % devices) for i in range(devices)])
        return block, new, total, weighted

    start = (
        kv,
        jnp.full((CAP, 4), NEG, F32),
        jnp.zeros((CAP, 4), F32),
        jnp.zeros((CAP, 4, HD), F32),
    )
    _, _, total, weighted = lax.fori_loop(0, devices, step, start)
    a = (weighted / total[..., None]).reshape(CAP, 4 * HD).astype(BF)
    part = jnp.dot(a, wout, preferred_element_type=F32).astype(BF)
    return [lax.dynamic_slice_in_dim(part, ((y + k) % 4) * 256, 256, 1) for k in range(4)]


def mix_kernel(len_ref, skip_ref, p0, p1, p2, p3, mixed_ref, tail_ref):
    byte_rows = skip_ref.shape[0]
    lengths = len_ref[...].astype(F32)
    inner = p0[...].astype(F32) + p1[...].astype(F32) + p2[...].astype(F32) + p3[...].astype(F32)
    i, j = iota((CAP, CAP), 0), iota((CAP, CAP), 1)
    column = jnp.sum(jnp.where(i == j, lengths, 0.0), axis=1, keepdims=True)
    start = jnp.sum(jnp.where(i < j, column, 0.0), axis=0, keepdims=True)
    at = iota((byte_rows, CAP), 0).astype(F32)
    hot = jnp.where((at >= start) & (at < start + lengths), 1.0, 0.0).astype(BF)
    up = jnp.dot(hot, inner.astype(BF), preferred_element_type=F32)
    mixed = (skip_ref[...].astype(F32) + up).astype(BF)
    mixed_ref[...] = mixed
    tail_ref[...] = mixed[byte_rows - HALO :, :]


def mix(lengths, skip, parts):
    return pl.pallas_call(
        mix_kernel,
        in_specs=[vmem()] * 6,
        out_specs=[vmem()] * 2,
        out_shape=[
            jax.ShapeDtypeStruct(skip.shape, BF),
            jax.ShapeDtypeStruct((HALO, skip.shape[1]), BF),
        ],
        compiler_params=params(),
        name="mix",
    )(lengths, skip, *parts)


def filtered(window, taps):
    rows = window.shape[0] - HALO
    total = jnp.zeros((rows, window.shape[1]), F32)
    lags = taps.shape[0]
    for r in range(8):
        moved = window[8 - r : rows + HALO - r, :]
        for lag in range(r, lags, 8):
            low = HALO - 8 - (lag - r)
            total += taps[lag : lag + 1, :] * moved[low : low + rows, :]
    return (window[HALO:, :] + total / (1.0 + jnp.exp(-total))).astype(BF)


def conv_kernel(mixed_ref, taps_ref, out_ref, ext):
    byte_rows, channels = mixed_ref.shape
    ext[:HALO, :] = jnp.zeros((HALO, channels), F32)
    ext[HALO:, :] = mixed_ref[...].astype(F32)
    block = 128
    lags = taps_ref.shape[0]

    for first in range(0, byte_rows, block):
        for low in range(0, channels, 128):
            part = slice(low, low + 128)
            total = jnp.zeros((block, 128), F32)
            for lag in range(lags):
                start = first + HALO - lag
                total += taps_ref[lag : lag + 1, part] * ext[start : start + block, part]
            here = ext[first + HALO : first + HALO + block, part]
            silu = total / (1.0 + jnp.exp(-total))
            out_ref[first : first + block, part] = (here + silu).astype(BF)


def rim_kernel(given_hbm, rim_ref, mixed_ref, taps_ref, out_hbm, rows, sem):
    del given_hbm
    for low in range(0, mixed_ref.shape[1], 128):
        part = slice(low, low + 128)
        window = jnp.concatenate([rim_ref[:, part], mixed_ref[:HALO, part]], axis=0).astype(F32)
        rows[:, part] = filtered(window, taps_ref[:, part])
    copy = pltpu.make_async_copy(rows, out_hbm.at[pl.ds(0, HALO)], sem)
    copy.start()
    copy.wait()


def convolve(mixed, taps):
    return pl.pallas_call(
        conv_kernel,
        in_specs=[vmem()] * 2,
        out_specs=vmem(),
        out_shape=jax.ShapeDtypeStruct(mixed.shape, BF),
        scratch_shapes=[pltpu.VMEM((HALO + mixed.shape[0], mixed.shape[1]), F32)],
        compiler_params=params(),
        cost_estimate=pl.CostEstimate(
            flops=2 * mixed.size * taps.shape[0], bytes_accessed=16 * mixed.size, transcendentals=0
        ),
        name="convolve",
    )(mixed, taps)


def first_rows(given, rim, mixed, taps):
    return pl.pallas_call(
        rim_kernel,
        in_specs=[anywhere()] + [vmem()] * 3,
        out_specs=anywhere(),
        out_shape=jax.ShapeDtypeStruct(given.shape, BF),
        input_output_aliases={0: 0},
        scratch_shapes=[pltpu.VMEM((HALO, mixed.shape[1]), BF), pltpu.SemaphoreType.DMA],
        compiler_params=params(),
        name="first_rows",
    )(given, rim, mixed, taps)


def seq_permute(value, move):
    pairs = []
    for z in range(NZ):
        for x in range(NX):
            for core in range(2):
                tz, tx, tc = move(z, x, core)
                target = ((tz % NZ) * NX + tx % NX) * 2 + tc
                pairs.append(((z * NX + x) * 2 + core, target))
    return lax.ppermute(value, "seq", pairs)


def along_x(value, steps):
    return seq_permute(value, lambda z, x, c: (z, x + steps, c))


def round_z(value):
    return seq_permute(value, lambda z, x, c: (z + 1 - 2 * c, x, c))


def swap(value):
    return seq_permute(value, lambda z, x, c: (z, x, 1 - c))


def per_device(enc, span_len, skip, gain, wq, wk, wv, wout, taps):
    seq = lax.axis_index("seq")
    y = lax.axis_index("section")
    index = jnp.stack([seq // (2 * NX), (seq // 2) % NX, seq % 2, y]).astype(jnp.int32)
    kv, x, scale = pool(span_len, enc, gain.reshape(1, -1), wk, wv)
    across = along_x(kv, 2)
    column = [kv, along_x(kv, 1), along_x(kv, -1), across]
    plane = compact(index, column + [swap(v) for v in column])
    first, q = lax.optimization_barrier((round_z(plane), query(x, wq, scale)))
    came = [first]
    came.append(round_z(first))
    near = attend_near(index, q, [plane] + came + [swap(piece) for piece in came])
    third, (*state, info) = lax.optimization_barrier((round_z(came[-1]), near))
    far = round_z(lax.dynamic_slice_in_dim(third, (seq % 2) * HALF, UPPER, 0))
    more = attend_more(index, q, third, swap(third), state, info)
    far, (*state, info) = lax.optimization_barrier((far, more))
    parts, crowded = attend_far(index, info, q, wout, far, swap(far), state)
    parts = lax.cond(
        crowded > 0, lambda _: attend_any(kv, q, span_len, wout, y), lambda given: given, parts
    )
    sent = [
        lax.ppermute(parts[k], "section", [(i, (i + k) % 4) for i in range(4)]) for k in (2, 1, 3)
    ]
    mixed, tail = mix(span_len, skip, [parts[0]] + sent)
    rim = lax.ppermute(tail, "seq", [(i, i + 1) for i in range(2 * NX * NZ - 1)])
    return first_rows(convolve(mixed, taps), rim, mixed, taps)


def solution(mesh):
    return jax.shard_map(
        per_device,
        mesh=mesh,
        in_specs=(
            P("seq", None),
            P("seq", None),
            P("seq", "section"),
            P(),
            P(None, "section"),
            P(None, "section"),
            P(None, "section"),
            P("section", None),
            P(None, "section"),
        ),
        out_specs=P("seq", "section"),
        check_vma=False,
    )
```
